32 devices in a mesh: head: 4 (over y, x), ctx: 8 (over z, core).
Axes of the slice: x: 2, y: 2, z: 4, core: 2. Of those that a mesh axis runs over, the one named last changes fastest.
Arguments:
- query: bfloat16 [8, 512, 4096], P('ctx', 'head'), may hold values from -6 to 6
- keys: bfloat16 [8, 512, 4096], P('ctx', 'head'), may hold values from -6 to 6
- values: bfloat16 [8, 512, 4096], P('ctx', 'head'), may hold values from -6 to 6
- grad_out: bfloat16 [8, 512, 4096], P('ctx', 'head'), may hold values from -6 to 6
Outputs:
- grad_q: bfloat16 [8, 512, 4096], P('ctx', None, 'head')
- grad_k: bfloat16 [8, 512, 4096], P('ctx', None, 'head')
- grad_v: bfloat16 [8, 512, 4096], P('ctx', None, 'head')
The draws below stay inside these ranges and needn't reach their ends.
All inputs are finite; a program needn't handle non-finite values.
Results may differ from the reference program's by a relative error of at most 0.0049.
Values may be sent and summed in bfloat16 or wider, within the bound.
No kernel may reach another device: no remote copies, remote signals or barrier semaphores. Data moves between devices by JAX's collectives and lax.ppermute only.
A program may use at most 192 MiB of HBM per device.

```python
import jax
import jax.numpy as jnp
from jax import lax

HD = 128
BLOCK = 512
TOK_DEV = 512
HEADS = 32
WIDTH = 4096
SPANS = 8
LENGTH = 4096


def block_scale(own_key, shape, split, low, largest):
    factor_of, own = 1.0, jax.random.fold_in(own_key, 6)
    for axis_at, shards_of in split:
        steps = jnp.exp(jax.random.uniform(jax.random.fold_in(own, axis_at), (shards_of,), jnp.float32, low / len(split), largest / len(split)))
        factor_of = factor_of * jnp.repeat(steps, shape[axis_at] // shards_of).reshape([-1 if axis == axis_at else 1 for axis in range(len(shape))])
    return factor_of


def scatter_about(key, dims, deviation, bound, split=(), held_as=jnp.bfloat16):
    loudness = block_scale(key, dims, split, -0.22, 0.18) if split else 1.0
    values = jax.random.normal(key, dims, jnp.float32) * deviation * loudness
    return jnp.minimum(jnp.maximum(values, -bound), bound).astype(held_as)


def setup_inputs(seed: int = 0) -> dict:
    splits = jax.random.split(jax.random.key(seed), 5)
    return {
        "query": scatter_about(splits[0], (SPANS, TOK_DEV, WIDTH), 1.0, 6.0, ((0, 8), (1, 4))),
        "keys": scatter_about(splits[1], (SPANS, TOK_DEV, WIDTH), 1.0, 6.0, ((0, 8), (1, 4))),
        "values": scatter_about(splits[2], (SPANS, TOK_DEV, WIDTH), 1.0, 6.0, ((0, 8), (1, 4))),
        "grad_out": scatter_about(splits[3], (SPANS, TOK_DEV, WIDTH), 1.0, 6.0, ((0, 8), (1, 4))),
    }


def reference(query, keys, values, grad_out):
    factor = (HD * LENGTH) ** -0.5
    count = LENGTH // BLOCK

    def split_heads(x):
        return x.reshape(count, BLOCK, HEADS, HD)

    query_blocks = split_heads(query)
    keys_blocks = split_heads(keys)
    values_blocks = split_heads(values)
    grads_blocks = split_heads(grad_out)

    def own_states(item):
        qpart, kpart, vpart, gpart = item
        key_part = jnp.einsum('cha,chb->hab', kpart.astype(jnp.float32), vpart.astype(jnp.float32))
        query_part = jnp.einsum('cha,chb->hab', qpart.astype(jnp.float32), gpart.astype(jnp.float32))
        return key_part, query_part

    key_own, query_own = lax.map(own_states, (query_blocks, keys_blocks, values_blocks, grads_blocks))
    key_states = jnp.cumsum(key_own, 0) - key_own
    query_states = jnp.sum(query_own, 0)[None] - jnp.cumsum(query_own, 0)
    causal = jnp.tril(jnp.ones((BLOCK, BLOCK), jnp.bool_))

    def block_grads(item):
        qpart, kpart, vpart, gpart, kstate, qstate = item
        key_rounded = kstate.astype(jnp.bfloat16).astype(jnp.float32)
        query_rounded = qstate.astype(jnp.bfloat16).astype(jnp.float32)
        qf = qpart.astype(jnp.float32)
        kf = kpart.astype(jnp.float32)
        vf = vpart.astype(jnp.float32)
        gf = gpart.astype(jnp.float32)
        out_scores = jnp.einsum('phd,thd->hpt', gf, vf) * factor
        out_scores = jnp.where(causal[None], out_scores, 0.0).astype(jnp.bfloat16).astype(jnp.float32)
        key_scores = jnp.einsum('phd,thd->hpt', qf, kf) * factor
        key_scores = jnp.where(causal[None], key_scores, 0.0).astype(jnp.bfloat16).astype(jnp.float32)
        grad_query = jnp.einsum('hpt,thd->phd', out_scores, kf) + factor * jnp.einsum('phe,hde->phd', gf, key_rounded)
        grad_key = jnp.einsum('hpt,phd->thd', out_scores, qf) + factor * jnp.einsum('the,hde->thd', vf, query_rounded)
        grad_value = jnp.einsum('hpt,phe->the', key_scores, gf) + factor * jnp.einsum('thd,hde->the', kf, query_rounded)
        return grad_query.astype(jnp.bfloat16), grad_key.astype(jnp.bfloat16), grad_value.astype(jnp.bfloat16)

    grad_query, grad_key, grad_value = lax.map(block_grads, (query_blocks, keys_blocks, values_blocks, grads_blocks, key_states, query_states))
    shape = (SPANS, TOK_DEV, WIDTH)
    return grad_query.reshape(shape), grad_key.reshape(shape), grad_value.reshape(shape)
```

```python
import functools

import jax
import jax.numpy as jnp
from jax import lax
from jax.experimental import pallas as pl
from jax.experimental.pallas import tpu as pltpu
from jax.sharding import PartitionSpec as P

HD = 128
TILE = 256
F32 = jnp.float32
BF16 = jnp.bfloat16
PARAMS = pltpu.CompilerParams(vmem_limit_bytes=40 * 1024 * 1024)


def dot(a, b, contract):
    return lax.dot_general(a, b, ((contract[:1], contract[1:]), ((), ())), preferred_element_type=F32)


def cost(flops, count):
    return pl.CostEstimate(flops=10**10, bytes_accessed=2 * count, transcendentals=0)


def target_of(me, step, parts):
    if parts & (parts - 1) == 0:
        return me ^ step
    return (me + step) % parts


def source_of(me, step, parts):
    if parts & (parts - 1) == 0:
        return me ^ step
    return (me + parts - step) % parts


def send(value, axis, target):
    count = lax.axis_size(axis)
    return lax.ppermute(value, axis, [(index, target(index)) for index in range(count)])


def pack_kernel(parts, heads, chunks, *refs):
    inputs, outputs, (loaded, staged, load_sem, store_sem) = refs[:4], refs[4:-4], refs[-4:]
    me = lax.axis_index("head")
    group = heads * HD

    def load(step, tensor):
        start = pl.multiple_of(target_of(me, step, parts) * group, group)
        return pltpu.make_async_copy(
            inputs[tensor].at[0, :, pl.ds(start, group)],
            loaded.at[step, tensor],
            load_sem.at[step, tensor],
        )

    order = list(range(1, parts)) + [0]
    for step in order:
        for tensor in range(4):
            load(step, tensor).start()
    last = len(chunks) - 1
    stores = []
    for step in order:
        for tensor in range(4):
            load(step, tensor).wait()
        at = 0
        head = 0
        for chunk, count in enumerate(chunks):
            first = at
            for _ in range(count):
                for tensor in range(4):
                    staged[step, at] = loaded[step, tensor, :, head * HD : (head + 1) * HD]
                    at += 1
                head += 1
            if chunk == 0:
                for late in range(heads - chunks[last], heads):
                    query, keys, values, grads = (
                        loaded[step, tensor, :, late * HD : (late + 1) * HD] for tensor in range(4)
                    )
                    staged[step, at] = dot(values, keys, (0, 0)).astype(BF16)
                    staged[step, at + 1] = dot(query, grads, (0, 0)).astype(BF16)
                    at += 2
            store = pltpu.make_async_copy(
                staged.at[step, first:at],
                outputs[chunk * parts + step],
                store_sem.at[step, chunk],
            )
            store.start()
            stores.append(store)
    for store in stores:
        store.wait()


@jax.named_scope("pack")
def pack(arrays, parts, heads, chunks):
    _, rows, full = arrays[0].shape
    units = [4 * count for count in chunks]
    units[0] += 2 * chunks[-1]
    out = [jax.ShapeDtypeStruct((unit, rows, HD), BF16) for unit in units for _ in range(parts)]
    flat = pl.pallas_call(
        functools.partial(pack_kernel, parts, heads, chunks),
        in_specs=[pl.BlockSpec(memory_space=pltpu.HBM)] * 4,
        out_specs=[pl.BlockSpec(memory_space=pl.ANY)] * len(out),
        out_shape=out,
        scratch_shapes=[
            pltpu.VMEM((parts, 4, rows, heads * HD), BF16),
            pltpu.VMEM((parts, sum(units), rows, HD), BF16),
            pltpu.SemaphoreType.DMA((parts, 4)),
            pltpu.SemaphoreType.DMA((parts, len(chunks))),
        ],
        compiler_params=PARAMS,
        cost_estimate=cost(0, 8 * rows * full),
    )(*[pltpu.with_memory_space_constraint(value, pltpu.HBM) for value in arrays])
    return [flat[chunk * parts : (chunk + 1) * parts] for chunk in range(len(chunks))]


def state_kernel(parts, heads, extra, *refs):
    inputs, out = refs[:parts], refs[-1]
    for head in range(heads):
        query, keys, values, grads = (
            jnp.concatenate([ref[4 * head + tensor] for ref in inputs], 0) for tensor in range(4)
        )
        out[0, head] = dot(values, keys, (0, 0))
        out[1, head] = dot(query, grads, (0, 0))
    for late in range(extra):
        for state in range(2):
            at = 4 * heads + 2 * late + state
            out[state, heads + late] = sum(ref[at].astype(F32) for ref in inputs)


@jax.named_scope("own_states")
def own_states(received, heads, extra, before):
    parts = len(received)
    rows = received[0].shape[1]
    return pl.pallas_call(
        functools.partial(state_kernel, parts, heads, extra),
        in_specs=[pl.BlockSpec(memory_space=pltpu.VMEM)] * parts
        + [pl.BlockSpec(memory_space=pl.ANY)] * len(before),
        out_shape=jax.ShapeDtypeStruct((2, heads + extra, HD, HD), F32),
        compiler_params=PARAMS,
        cost_estimate=cost(4 * heads * parts * rows * HD * HD, parts * received[0].size),
    )(*received, *before)


def chip_kernel(chips, own, partner, *outputs):
    chip = lax.axis_index("ctx") // 2
    keys = (own[0] + partner[0]).astype(BF16)
    query = (own[1] + partner[1]).astype(BF16)
    for step in range(1, chips):
        outputs[step - 1][...] = jnp.where(chip + step < chips, keys, query)


@jax.named_scope("chip_states")
def chip_states(own, partner, chips):
    shape = own.shape[1:]
    return pl.pallas_call(
        functools.partial(chip_kernel, chips),
        out_shape=[jax.ShapeDtypeStruct(shape, BF16)] * (chips - 1),
        compiler_params=PARAMS,
        cost_estimate=cost(0, 4 * own.size),
    )(own, partner)


def other_states(own):
    spans = lax.axis_size("ctx")
    chips = spans // 2
    if spans % 2 or chips > 4:
        return [lax.all_gather(own.astype(BF16), "ctx")]
    partner = send(own, "ctx", lambda index: index ^ 1)
    sums = chip_states(own, partner, chips)
    return [partner] + [
        send(value, "ctx", lambda index: (index + 2 * step) % spans)
        for step, value in enumerate(sums, 1)
    ]


def read_states(refs, spans, head):
    me = lax.axis_index("ctx")
    zero = jnp.zeros((HD, HD), F32)
    if len(refs) == 1:

        def add(span, totals):
            keys, query = totals
            keys = keys + jnp.where(span < me, refs[0][span, 0, head].astype(F32), 0.0)
            query = query + jnp.where(span > me, refs[0][span, 1, head].astype(F32), 0.0)
            return keys, query

        return lax.fori_loop(0, spans, add, (zero, zero))
    partner, others = refs[0], refs[1:]
    chip, core = me // 2, me % 2
    keys = jnp.where(core == 1, partner[0, head], 0.0)
    query = jnp.where(core == 0, partner[1, head], 0.0)
    for step, ref in enumerate(others, 1):
        part = ref[head].astype(F32)
        keys = keys + jnp.where(chip >= step, part, 0.0)
        query = query + jnp.where(chip < step, part, 0.0)
    return keys, query


def grads_kernel(parts, spans, factor, offset, counts, *refs):
    received, states = refs[: counts[0]], refs[counts[0] : counts[0] + counts[1]]
    grad_query, grad_key, grad_value, ordered = refs[-4:]
    me = lax.axis_index("head")
    rows = received[0].shape[1]
    head = pl.program_id(0)
    for step, ref in enumerate(received):
        place = source_of(me, step, parts)
        for tensor in range(4):
            ordered[tensor, place] = ref[tensor]
    key_state, query_state = read_states(states, spans, head + offset)
    key_state = key_state.astype(BF16)
    query_turned = query_state.T.astype(BF16)
    query_state = query_state.astype(BF16)
    length = parts * rows
    tiles = length // TILE
    query, keys, values, grads = (
        ordered[tensor].reshape(tiles, TILE, HD) for tensor in range(4)
    )
    row = lax.broadcasted_iota(jnp.int32, (TILE, TILE), 0)
    column = lax.broadcasted_iota(jnp.int32, (TILE, TILE), 1)

    def scores(a, b, keep):
        value = dot(a, b, (1, 1))
        if keep is not None:
            value = jnp.where(keep, value, 0.0)
        return value.astype(BF16)

    def total(lefts, rights):
        value = dot(jnp.concatenate(lefts, 1), jnp.concatenate(rights, 0), (1, 0))
        return (value * factor).astype(BF16)

    for i in range(tiles):
        at = slice(i * TILE, (i + 1) * TILE)
        low = [scores(grads[i], values[j], column <= row if i == j else None) for j in range(i + 1)]
        grad_query[0, at] = total(
            low + [grads[i]], [keys[j] for j in range(i + 1)] + [key_state]
        )
        high = [scores(values[i], grads[j], row <= column if i == j else None) for j in range(i, tiles)]
        grad_key[0, at] = total(
            high + [values[i]], [query[j] for j in range(i, tiles)] + [query_turned]
        )
        high = [scores(keys[i], query[j], row <= column if i == j else None) for j in range(i, tiles)]
        grad_value[0, at] = total(
            high + [keys[i]], [grads[j] for j in range(i, tiles)] + [query_state]
        )


@jax.named_scope("gradients")
def gradients(received, states, offset, held, first, heads, group, factor):
    parts = len(received)
    rows = received[0].shape[1]
    spans = lax.axis_size("ctx")
    length = parts * rows
    kept = len(held)
    counts = (parts, len(states))
    return pl.pallas_call(
        functools.partial(grads_kernel, parts, spans, factor, offset, counts),
        grid=(heads,),
        in_specs=[pl.BlockSpec((4, rows, HD), lambda h: (h, 0, 0))] * parts
        + [pl.BlockSpec(value.shape, lambda h, rank=value.ndim: (0,) * rank) for value in states]
        + [pl.BlockSpec(memory_space=pl.ANY)] * kept,
        out_specs=[pl.BlockSpec((1, length, HD), lambda h: (0, 0, first + h))] * 3,
        out_shape=[jax.ShapeDtypeStruct((1, length, group), BF16)] * 3,
        scratch_shapes=[pltpu.VMEM((4, parts, rows, HD), BF16)],
        input_output_aliases={sum(counts) + index: index for index in range(kept)},
        compiler_params=PARAMS,
        cost_estimate=cost(
            heads * (8 * length * length * HD + 6 * length * HD * HD), 7 * heads * length * HD
        ),
    )(*received, *states, *held)


def shards(query, keys, values, grad_out):
    parts = lax.axis_size("head")
    spans = lax.axis_size("ctx")
    _, rows, full = query.shape
    group = full // parts
    heads = group // HD
    factor = (HD * rows * parts * spans) ** -0.5
    late = max(1, heads // 4)
    middle = (heads - late) // 2
    chunks = [heads - late - middle, middle, late]
    packed = pack((query, keys, values, grad_out), parts, heads, chunks)
    received = [
        [values[0]]
        + [
            send(values[step], "head", lambda index: target_of(index, step, parts))
            for step in range(1, parts)
        ]
        for values in packed
    ]
    early = other_states(own_states(received[0], chunks[0], late, []))
    second = other_states(own_states(received[1], middle, 0, early[1:]))
    held = gradients(received[0], early, 0, (), 0, chunks[0], group, factor)
    held = gradients(received[1], second, 0, held, chunks[0], middle, group, factor)
    held = gradients(received[2], early, chunks[0], held, heads - late, late, group, factor)
    return tuple(held)


def solution(mesh):
    spec = P("ctx", "head", None)
    out = P("ctx", None, "head")
    return jax.shard_map(
        shards, mesh=mesh, in_specs=(spec,) * 4, out_specs=(out,) * 3, check_vma=False
    )
```

```python
import functools

import jax
import jax.numpy as jnp
from jax import lax
from jax.experimental import pallas as pl
from jax.experimental.pallas import tpu as pltpu
from jax.sharding import PartitionSpec as P

HD = 128
TILE = 256
F32 = jnp.float32
BF16 = jnp.bfloat16
PARAMS = pltpu.CompilerParams(vmem_limit_bytes=40 * 1024 * 1024)


def dot(a, b, contract):
    return lax.dot_general(a, b, ((contract[:1], contract[1:]), ((), ())), preferred_element_type=F32)


def in_hbm(arrays):
    return [pltpu.with_memory_space_constraint(value, pltpu.HBM) for value in arrays]


def cost(flops, count):
    return pl.CostEstimate(flops=flops, bytes_accessed=2 * count, transcendentals=0)


def target_of(me, step, parts):
    if parts & (parts - 1) == 0:
        return me ^ step
    return (me + step) % parts


def source_of(me, step, parts):
    if parts & (parts - 1) == 0:
        return me ^ step
    return (me + parts - step) % parts


def send(value, axis, target):
    count = lax.axis_size(axis)
    return lax.ppermute(value, axis, [(index, target(index)) for index in range(count)])


def copy_heads(inputs, parts, heads, step, head, count, target, at, sem):
    column = (target_of(lax.axis_index("head"), step, parts) * heads + head) * HD
    return [
        pltpu.make_async_copy(
            inputs[tensor].at[0, :, pl.ds(pl.multiple_of(column + index * HD, HD), HD)],
            target.at[at + 4 * index + tensor],
            sem,
        )
        for index in range(count)
        for tensor in range(4)
    ]


def first_kernel(parts, heads, count, late, *refs):
    inputs, outputs, (loaded, load_sem, copy_sem) = refs[:4], refs[4 : 3 + parts], refs[-3:]
    steps = range(1, parts)
    loads = [
        copy_heads(inputs, parts, heads, step, heads - late, late, loaded.at[step - 1], 0, load_sem.at[step - 1])
        for step in steps
    ]
    copies = [
        copy_heads(inputs, parts, heads, step, 0, count, outputs[step - 1], 0, copy_sem.at[step - 1])
        for step in steps
    ]
    for copy in sum(loads, []) + sum(copies, []):
        copy.start()
    for step in steps:
        for copy in loads[step - 1]:
            copy.wait()
        for index in range(late):
            query, keys, values, grads = (loaded[step - 1, 4 * index + tensor] for tensor in range(4))
            at = 4 * count + 2 * index
            outputs[step - 1][at] = dot(values, keys, (0, 0)).astype(BF16)
            outputs[step - 1][at + 1] = dot(query, grads, (0, 0)).astype(BF16)
    for copy in sum(copies, []):
        copy.wait()


@jax.named_scope("pack")
def pack_first(arrays, parts, heads, count, late):
    _, rows, full = arrays[0].shape
    units = 4 * count + 2 * late
    return pl.pallas_call(
        functools.partial(first_kernel, parts, heads, count, late),
        in_specs=[pl.BlockSpec(memory_space=pltpu.HBM)] * 4,
        out_specs=[pl.BlockSpec(memory_space=pltpu.VMEM)] * (parts - 1),
        out_shape=[jax.ShapeDtypeStruct((units, rows, HD), BF16)] * (parts - 1),
        scratch_shapes=[
            pltpu.VMEM((parts - 1, 4 * late, rows, HD), BF16),
            pltpu.SemaphoreType.DMA((parts - 1,)),
            pltpu.SemaphoreType.DMA((parts - 1,)),
        ],
        compiler_params=PARAMS,
        cost_estimate=cost(1000, 1024),
    )(*in_hbm(arrays))


def rest_kernel(parts, heads, chunks, *refs):
    inputs, outputs, (loaded, load_sem, copy_sem) = refs[:4], refs[4:-3], refs[-3:]
    late = chunks[-1]
    loads = copy_heads(inputs, parts, heads, 0, heads - late, late, loaded, 0, load_sem)
    copies, head = [], 0
    for chunk, count in enumerate(chunks):
        for step in range(parts):
            if chunk or not step:
                target = outputs[0] if not chunk else outputs[1 + (chunk - 1) * parts + step]
                copies += copy_heads(inputs, parts, heads, step, head, count, target, 0, copy_sem)
        head += count
    for copy in loads + copies:
        copy.start()
    for copy in loads:
        copy.wait()
    for index in range(late):
        query, keys, values, grads = (loaded[4 * index + tensor] for tensor in range(4))
        at = 4 * chunks[0] + 2 * index
        outputs[0][at] = dot(values, keys, (0, 0)).astype(BF16)
        outputs[0][at + 1] = dot(query, grads, (0, 0)).astype(BF16)
    for copy in copies:
        copy.wait()


@jax.named_scope("pack")
def pack_rest(arrays, parts, heads, chunks):
    _, rows, full = arrays[0].shape
    units = [4 * chunks[0] + 2 * chunks[-1]] + [4 * count for count in chunks[1:] for _ in range(parts)]
    flat = pl.pallas_call(
        functools.partial(rest_kernel, parts, heads, chunks),
        in_specs=[pl.BlockSpec(memory_space=pltpu.HBM)] * 4,
        out_specs=[pl.BlockSpec(memory_space=pltpu.VMEM)] * len(units),
        out_shape=[jax.ShapeDtypeStruct((unit, rows, HD), BF16) for unit in units],
        scratch_shapes=[
            pltpu.VMEM((4 * chunks[-1], rows, HD), BF16),
            pltpu.SemaphoreType.DMA,
            pltpu.SemaphoreType.DMA,
        ],
        compiler_params=PARAMS,
        cost_estimate=cost(1000, 1024),
    )(*in_hbm(arrays))
    return flat[0], [flat[1 + chunk * parts : 1 + (chunk + 1) * parts] for chunk in range(len(chunks) - 1)]


def state_kernel(parts, heads, extra, *refs):
    inputs, out = refs[:parts], refs[-1]
    for head in range(heads):
        query, keys, values, grads = (
            jnp.concatenate([ref[4 * head + tensor] for ref in inputs], 0) for tensor in range(4)
        )
        out[0, head] = dot(values, keys, (0, 0))
        out[1, head] = dot(query, grads, (0, 0))
    for late in range(extra):
        for state in range(2):
            at = 4 * heads + 2 * late + state
            out[state, heads + late] = sum(ref[at].astype(F32) for ref in inputs)


@jax.named_scope("own_states")
def own_states(received, heads, extra, before):
    parts = len(received)
    rows = received[0].shape[1]
    return pl.pallas_call(
        functools.partial(state_kernel, parts, heads, extra),
        in_specs=[pl.BlockSpec(memory_space=pltpu.VMEM)] * parts
        + [pl.BlockSpec(memory_space=pl.ANY)] * len(before),
        out_shape=jax.ShapeDtypeStruct((2, heads + extra, HD, HD), F32),
        compiler_params=PARAMS,
        cost_estimate=cost(1000, 1024),
    )(*received, *before)


def chip_kernel(chips, own, partner, *outputs):
    chip = lax.axis_index("ctx") // 2
    keys = (own[0] + partner[0]).astype(BF16)
    query = (own[1] + partner[1]).astype(BF16)
    for step in range(1, chips):
        outputs[step - 1][...] = jnp.where(chip + step < chips, keys, query)


@jax.named_scope("chip_states")
def chip_states(own, partner, chips):
    shape = own.shape[1:]
    return pl.pallas_call(
        functools.partial(chip_kernel, chips),
        out_shape=[jax.ShapeDtypeStruct(shape, BF16)] * (chips - 1),
        compiler_params=PARAMS,
        cost_estimate=cost(10**10, 1024),
    )(own, partner)


def other_states(own):
    spans = lax.axis_size("ctx")
    chips = spans // 2
    if spans % 2 or chips > 4:
        return [lax.all_gather(own.astype(BF16), "ctx")]
    partner = send(own, "ctx", lambda index: index ^ 1)
    sums = chip_states(own, partner, chips)
    return [partner] + [
        send(value, "ctx", lambda index: (index + 2 * step) % spans)
        for step, value in enumerate(sums, 1)
    ]


def read_states(refs, spans, head):
    me = lax.axis_index("ctx")
    zero = jnp.zeros((HD, HD), F32)
    if len(refs) == 1:

        def add(span, totals):
            keys, query = totals
            keys = keys + jnp.where(span < me, refs[0][span, 0, head].astype(F32), 0.0)
            query = query + jnp.where(span > me, refs[0][span, 1, head].astype(F32), 0.0)
            return keys, query

        return lax.fori_loop(0, spans, add, (zero, zero))
    partner, others = refs[0], refs[1:]
    chip, core = me // 2, me % 2
    keys = jnp.where(core == 1, partner[0, head], 0.0)
    query = jnp.where(core == 0, partner[1, head], 0.0)
    for step, ref in enumerate(others, 1):
        part = ref[head].astype(F32)
        keys = keys + jnp.where(chip >= step, part, 0.0)
        query = query + jnp.where(chip < step, part, 0.0)
    return keys, query


def grads_kernel(parts, spans, factor, offset, first, counts, *refs):
    received, states = refs[: counts[0]], refs[counts[0] : counts[0] + counts[1]]
    outputs, (ordered, staged, sem) = refs[-6:-3], refs[-3:]
    heads = ordered.shape[0]
    me = lax.axis_index("head")
    rows = received[0].shape[1]
    length = parts * rows
    tiles = length // TILE
    row = lax.broadcasted_iota(jnp.int32, (TILE, TILE), 0)
    column = lax.broadcasted_iota(jnp.int32, (TILE, TILE), 1)
    low, high = column <= row, row <= column

    def scores(a, b, keep):
        value = dot(a, b, (1, 1))
        if keep is not None:
            value = jnp.where(keep, value, 0.0)
        return value.astype(BF16)

    def total(lefts, rights):
        value = dot(jnp.concatenate(lefts, 1), jnp.concatenate(rights, 0), (1, 0))
        return (value * factor).astype(BF16)

    copies = []
    for head in range(heads):
        for step, ref in enumerate(received):
            place = source_of(me, step, parts)
            for tensor in range(4):
                ordered[head, tensor, place] = ref[4 * head + tensor]
        key_state, query_state = read_states(states, spans, head + offset)
        key_state = key_state.astype(BF16)
        query_turned = query_state.T.astype(BF16)
        query_state = query_state.astype(BF16)
        query, keys, values, grads = (
            ordered[head, tensor].reshape(tiles, TILE, HD) for tensor in range(4)
        )
        for i in range(tiles):
            at = slice(i * TILE, (i + 1) * TILE)
            before, after = range(i + 1), range(i, tiles)
            staged[head, 0, at] = total(
                [scores(grads[i], values[j], low if i == j else None) for j in before] + [grads[i]],
                [keys[j] for j in before] + [key_state],
            )
            staged[head, 1, at] = total(
                [scores(values[i], grads[j], high if i == j else None) for j in after] + [values[i]],
                [query[j] for j in after] + [query_turned],
            )
            staged[head, 2, at] = total(
                [scores(keys[i], query[j], high if i == j else None) for j in after] + [keys[i]],
                [grads[j] for j in after] + [query_state],
            )
        for index, out in enumerate(outputs):
            copies.append(
                pltpu.make_async_copy(
                    staged.at[head, index],
                    out.at[0, :, pl.ds((first + head) * HD, HD)],
                    sem.at[head, index],
                )
            )
            copies[-1].start()
    for copy in copies:
        copy.wait()


@jax.named_scope("gradients")
def gradients(received, states, offset, held, first, heads, group, factor):
    parts = len(received)
    rows = received[0].shape[1]
    spans = lax.axis_size("ctx")
    length = parts * rows
    kept = len(held)
    counts = (parts, len(states))
    return pl.pallas_call(
        functools.partial(grads_kernel, parts, spans, factor, offset, first, counts),
        in_specs=[pl.BlockSpec(memory_space=pltpu.VMEM)] * sum(counts)
        + [pl.BlockSpec(memory_space=pltpu.HBM)] * kept,
        out_specs=[pl.BlockSpec(memory_space=pltpu.HBM)] * 3,
        out_shape=[jax.ShapeDtypeStruct((1, length, group), BF16)] * 3,
        scratch_shapes=[
            pltpu.VMEM((heads, 4, parts, rows, HD), BF16),
            pltpu.VMEM((heads, 3, length, HD), BF16),
            pltpu.SemaphoreType.DMA((heads, 3)),
        ],
        input_output_aliases={sum(counts) + index: index for index in range(kept)},
        compiler_params=PARAMS,
        cost_estimate=cost(1000, 1024),
    )(*received, *states, *held)


def shards(query, keys, values, grad_out):
    parts = lax.axis_size("head")
    spans = lax.axis_size("ctx")
    _, rows, full = query.shape
    group = full // parts
    heads = group // HD
    factor = (HD * rows * parts * spans) ** -0.5
    late = max(1, heads // 4)
    middle = (heads - late) // 2
    chunks = [heads - late - middle, middle, late]
    arrays = (query, keys, values, grad_out)
    first = pack_first(arrays, parts, heads, chunks[0], late)
    own, packed = pack_rest(arrays, parts, heads, chunks)

    def exchange(own, values):
        moved = {
            step: send(value, "head", lambda index: target_of(index, step, parts))
            for step, value in list(enumerate(values, 1))[1:] + [(1, values[0])]
        }
        return [own] + [moved[step] for step in range(1, parts)]

    received = [exchange(own, first)] + [exchange(values[0], values[1:]) for values in packed]
    early = other_states(own_states(received[0], chunks[0], late, []))
    second = other_states(own_states(received[1], middle, 0, early[1:]))
    held = gradients(received[0], early, 0, (), 0, chunks[0], group, factor)
    held = gradients(received[1], second, 0, held, chunks[0], middle, group, factor)
    held = gradients(received[2], early, chunks[0], held, heads - late, late, group, factor)
    return tuple(held)


def solution(mesh):
    spec = P("ctx", "head", None)
    out = P("ctx", None, "head")
    return jax.shard_map(
        shards, mesh=mesh, in_specs=(spec,) * 4, out_specs=(out,) * 3, check_vma=False
    )
```

```python
import functools

import jax
import jax.numpy as jnp
from jax import lax
from jax.experimental import pallas as pl
from jax.experimental.pallas import tpu as pltpu
from jax.sharding import PartitionSpec as P

HD = 128
TILE = 256
F32 = jnp.float32
BF16 = jnp.bfloat16
PARAMS = pltpu.CompilerParams(vmem_limit_bytes=40 * 1024 * 1024)


def dot(a, b, contract):
    return lax.dot_general(a, b, ((contract[:1], contract[1:]), ((), ())), preferred_element_type=F32)


def in_hbm(arrays):
    return [pltpu.with_memory_space_constraint(value, pltpu.HBM) for value in arrays]


def cost(flops, count):
    return pl.CostEstimate(flops=flops, bytes_accessed=2 * count, transcendentals=0)


def target_of(me, step, parts):
    if parts & (parts - 1) == 0:
        return me ^ step
    return (me + step) % parts


def source_of(me, step, parts):
    if parts & (parts - 1) == 0:
        return me ^ step
    return (me + parts - step) % parts


def steps_of(parts):
    return [0] + list(range(2, parts)) + [1]


def send(value, axis, target):
    count = lax.axis_size(axis)
    return lax.ppermute(value, axis, [(index, target(index)) for index in range(count)])


def copy_heads(inputs, parts, heads, step, head, count, target, at, sem):
    column = (target_of(lax.axis_index("head"), step, parts) * heads + head) * HD
    return [
        pltpu.make_async_copy(
            inputs[tensor].at[0, :, pl.ds(pl.multiple_of(column + index * HD, HD), HD)],
            target.at[at + 4 * index + tensor],
            sem,
        )
        for index in range(count)
        for tensor in range(4)
    ]


def first_kernel(parts, heads, count, late, *refs):
    inputs, outputs, (loaded, load_sem, copy_sem) = refs[:4], refs[4 : 3 + parts], refs[-3:]
    steps = range(1, parts)
    loads = [
        copy_heads(inputs, parts, heads, step, heads - late, late, loaded.at[step - 1], 0, load_sem.at[step - 1])
        for step in steps
    ]
    copies = [
        copy_heads(inputs, parts, heads, step, 0, count, outputs[step - 1], 0, copy_sem.at[step - 1])
        for step in steps
    ]
    for copy in sum(loads, []) + sum(copies, []):
        copy.start()
    for step in steps:
        for copy in loads[step - 1]:
            copy.wait()
        for index in range(late):
            query, keys, values, grads = (loaded[step - 1, 4 * index + tensor] for tensor in range(4))
            at = 4 * count + 2 * index
            outputs[step - 1][at] = dot(values, keys, (0, 0)).astype(BF16)
            outputs[step - 1][at + 1] = dot(query, grads, (0, 0)).astype(BF16)
    for copy in sum(copies, []):
        copy.wait()


@jax.named_scope("pack")
def pack_first(arrays, parts, heads, count, late):
    _, rows, full = arrays[0].shape
    units = 4 * count + 2 * late
    return pl.pallas_call(
        functools.partial(first_kernel, parts, heads, count, late),
        in_specs=[pl.BlockSpec(memory_space=pltpu.HBM)] * 4,
        out_specs=[pl.BlockSpec(memory_space=pltpu.VMEM)] * (parts - 1),
        out_shape=[jax.ShapeDtypeStruct((units, rows, HD), BF16)] * (parts - 1),
        scratch_shapes=[
            pltpu.VMEM((parts - 1, 4 * late, rows, HD), BF16),
            pltpu.SemaphoreType.DMA((parts - 1,)),
            pltpu.SemaphoreType.DMA((parts - 1,)),
        ],
        compiler_params=PARAMS,
        cost_estimate=cost(1000, 1024),
    )(*in_hbm(arrays))


def rest_kernel(parts, heads, chunks, *refs):
    inputs, outputs, (loaded, load_sem, copy_sem) = refs[:4], refs[4:-3], refs[-3:]
    late = chunks[-1]
    loads = copy_heads(inputs, parts, heads, 0, heads - late, late, loaded, 0, load_sem)
    copies, head = [], 0
    for chunk, count in enumerate(chunks):
        for step in range(parts):
            if chunk or not step:
                target = outputs[0] if not chunk else outputs[1 + (chunk - 1) * parts + step]
                copies += copy_heads(inputs, parts, heads, step, head, count, target, 0, copy_sem)
        head += count
    for copy in loads + copies:
        copy.start()
    for copy in loads:
        copy.wait()
    for index in range(late):
        query, keys, values, grads = (loaded[4 * index + tensor] for tensor in range(4))
        at = 4 * chunks[0] + 2 * index
        outputs[0][at] = dot(values, keys, (0, 0)).astype(BF16)
        outputs[0][at + 1] = dot(query, grads, (0, 0)).astype(BF16)
    for copy in copies:
        copy.wait()


@jax.named_scope("pack")
def pack_rest(arrays, parts, heads, chunks):
    _, rows, full = arrays[0].shape
    units = [4 * chunks[0] + 2 * chunks[-1]] + [4 * count for count in chunks[1:] for _ in range(parts)]
    flat = pl.pallas_call(
        functools.partial(rest_kernel, parts, heads, chunks),
        in_specs=[pl.BlockSpec(memory_space=pltpu.HBM)] * 4,
        out_specs=[pl.BlockSpec(memory_space=pltpu.VMEM)] * len(units),
        out_shape=[jax.ShapeDtypeStruct((unit, rows, HD), BF16) for unit in units],
        scratch_shapes=[
            pltpu.VMEM((4 * chunks[-1], rows, HD), BF16),
            pltpu.SemaphoreType.DMA,
            pltpu.SemaphoreType.DMA,
        ],
        compiler_params=PARAMS,
        cost_estimate=cost(1000, 1024),
    )(*in_hbm(arrays))
    return flat[0], [flat[1 + chunk * parts : 1 + (chunk + 1) * parts] for chunk in range(len(chunks) - 1)]


def state_kernel(parts, heads, extra, *refs):
    inputs, (out, give) = refs[:parts], refs[-2:]
    for head in range(heads):
        query, keys, values, grads = (
            jnp.concatenate([ref[4 * head + tensor] for ref in inputs], 0) for tensor in range(4)
        )
        out[0, head] = dot(values, keys, (0, 0))
        out[1, head] = dot(query, grads, (0, 0))
        give[:, head] = out[:, head].astype(BF16)
    for late in range(extra):
        for state in range(2):
            at = 4 * heads + 2 * late + state
            out[state, heads + late] = sum(ref[at].astype(F32) for ref in inputs)
        give[:, heads + late] = out[:, heads + late].astype(BF16)


@jax.named_scope("own_states")
def own_states(received, heads, extra, before):
    parts = len(received)
    rows = received[0].shape[1]
    return pl.pallas_call(
        functools.partial(state_kernel, parts, heads, extra),
        in_specs=[pl.BlockSpec(memory_space=pltpu.VMEM)] * parts
        + [pl.BlockSpec(memory_space=pl.ANY)] * len(before),
        out_shape=[jax.ShapeDtypeStruct((2, heads + extra, HD, HD), kind) for kind in (F32, BF16)],
        compiler_params=PARAMS,
        cost_estimate=cost(1000, 1024),
    )(*received, *before)


def chip_kernel(chips, own, partner, *outputs):
    chip = lax.axis_index("ctx") // 2
    keys = (own[0] + partner[0]).astype(BF16)
    query = (own[1] + partner[1]).astype(BF16)
    for step in range(1, chips):
        outputs[step - 1][...] = jnp.where(chip + step < chips, keys, query)


@jax.named_scope("chip_states")
def chip_states(own, partner, chips):
    shape = own.shape[1:]
    return pl.pallas_call(
        functools.partial(chip_kernel, chips),
        out_shape=[jax.ShapeDtypeStruct(shape, BF16)] * (chips - 1),
        compiler_params=PARAMS,
        cost_estimate=cost(1000, 1024),
    )(own, partner)


def other_states(own, give):
    spans = lax.axis_size("ctx")
    chips = spans // 2
    if spans % 2 or chips > 4:
        return [lax.all_gather(give, "ctx")]
    partner = send(give, "ctx", lambda index: index ^ 1)
    sums = chip_states(own, partner, chips)
    return [partner] + [
        send(value, "ctx", lambda index: (index + 2 * step) % spans)
        for step, value in enumerate(sums, 1)
    ]


def read_states(refs, spans, head):
    me = lax.axis_index("ctx")
    zero = jnp.zeros((HD, HD), F32)
    if len(refs) == 1:

        def add(span, totals):
            keys, query = totals
            keys = keys + jnp.where(span < me, refs[0][span, 0, head].astype(F32), 0.0)
            query = query + jnp.where(span > me, refs[0][span, 1, head].astype(F32), 0.0)
            return keys, query

        return lax.fori_loop(0, spans, add, (zero, zero))
    partner, others = refs[0], refs[1:]
    chip, core = me // 2, me % 2
    keys = jnp.where(core == 1, partner[0, head].astype(F32), 0.0)
    query = jnp.where(core == 0, partner[1, head].astype(F32), 0.0)
    for step, ref in enumerate(others, 1):
        part = ref[head].astype(F32)
        keys = keys + jnp.where(chip >= step, part, 0.0)
        query = query + jnp.where(chip < step, part, 0.0)
    return keys, query


def grads_kernel(parts, spans, factor, offset, first, counts, *refs):
    received, states = refs[: counts[0]], refs[counts[0] : counts[0] + counts[1]]
    outputs, token, (ordered, staged, sem) = refs[-7:-4], refs[-4], refs[-3:]
    heads = ordered.shape[0]
    me = lax.axis_index("head")
    rows = received[0].shape[1]
    length = parts * rows
    tiles = length // TILE
    row = lax.broadcasted_iota(jnp.int32, (TILE, TILE), 0)
    column = lax.broadcasted_iota(jnp.int32, (TILE, TILE), 1)
    low, high = column <= row, row <= column

    def scores(a, b, keep):
        value = dot(a, b, (1, 1))
        if keep is not None:
            value = jnp.where(keep, value, 0.0)
        return value.astype(BF16)

    def total(lefts, rights):
        value = dot(jnp.concatenate(lefts, 1), jnp.concatenate(rights, 0), (1, 0))
        return (value * factor).astype(BF16)

    copies = []
    for head in range(heads):
        for step, ref in zip(steps_of(parts), received):
            place = source_of(me, step, parts)
            for tensor in range(4):
                ordered[head, tensor, place] = ref[4 * head + tensor]
        key_state, query_state = read_states(states, spans, head + offset)
        key_state = key_state.astype(BF16)
        query_turned = query_state.T.astype(BF16)
        query_state = query_state.astype(BF16)
        query, keys, values, grads = (
            ordered[head, tensor].reshape(tiles, TILE, HD) for tensor in range(4)
        )
        for i in range(tiles):
            at = slice(i * TILE, (i + 1) * TILE)
            before, after = range(i + 1), range(i, tiles)
            staged[head, 0, at] = total(
                [scores(grads[i], values[j], low if i == j else None) for j in before] + [grads[i]],
                [keys[j] for j in before] + [key_state],
            )
            staged[head, 1, at] = total(
                [scores(values[i], grads[j], high if i == j else None) for j in after] + [values[i]],
                [query[j] for j in after] + [query_turned],
            )
            staged[head, 2, at] = total(
                [scores(keys[i], query[j], high if i == j else None) for j in after] + [keys[i]],
                [grads[j] for j in after] + [query_state],
            )
        for index, out in enumerate(outputs):
            copies.append(
                pltpu.make_async_copy(
                    staged.at[head, index],
                    out.at[0, :, pl.ds((first + head) * HD, HD)],
                    sem.at[head, index],
                )
            )
            copies[-1].start()
    for copy in copies:
        copy.wait()
    token[...] = jnp.zeros_like(token)


@jax.named_scope("gradients")
def gradients(received, states, offset, held, first, heads, group, factor):
    parts = len(received)
    rows = received[0].shape[1]
    length = parts * rows
    kept = len(held)
    counts = (parts, len(states))
    return pl.pallas_call(
        functools.partial(grads_kernel, parts, lax.axis_size("ctx"), factor, offset, first, counts),
        in_specs=[pl.BlockSpec(memory_space=pltpu.VMEM)] * sum(counts)
        + [pl.BlockSpec(memory_space=pltpu.HBM)] * kept,
        out_specs=[pl.BlockSpec(memory_space=pltpu.HBM)] * 3 + [pl.BlockSpec(memory_space=pltpu.VMEM)],
        out_shape=[jax.ShapeDtypeStruct((1, length, group), BF16)] * 3
        + [jax.ShapeDtypeStruct((8, HD), F32)],
        scratch_shapes=[
            pltpu.VMEM((heads, 4, parts, rows, HD), BF16),
            pltpu.VMEM((heads, 3, length, HD), BF16),
            pltpu.SemaphoreType.DMA((heads, 3)),
        ],
        input_output_aliases={sum(counts) + index: index for index in range(kept)},
        compiler_params=PARAMS,
        cost_estimate=cost(1000, 1024),
    )(*received, *states, *held)


def shards(query, keys, values, grad_out):
    parts = lax.axis_size("head")
    spans = lax.axis_size("ctx")
    _, rows, full = query.shape
    group = full // parts
    heads = group // HD
    factor = (HD * rows * parts * spans) ** -0.5
    late = max(1, heads // 4)
    middle = (heads - late) // 2
    chunks = [heads - late - middle, middle, late]
    arrays = (query, keys, values, grad_out)
    first = pack_first(arrays, parts, heads, chunks[0], late)
    own, packed = pack_rest(arrays, parts, heads, chunks)

    def exchange(own, values):
        return [own] + [
            send(values[step - 1], "head", lambda index: target_of(index, step, parts))
            for step in steps_of(parts)[1:]
        ]

    received = [exchange(own, first)] + [exchange(values[0], values[1:]) for values in packed]
    early = other_states(*own_states(received[0], chunks[0], late, []))
    *held, token = gradients(received[0], early, 0, (), 0, chunks[0], group, factor)
    second = other_states(*own_states(received[1], middle, 0, [token]))
    *held, _ = gradients(received[1], second, 0, held, chunks[0], middle, group, factor)
    *held, _ = gradients(received[2], early, chunks[0], held, heads - late, late, group, factor)
    return tuple(held)


def solution(mesh):
    spec = P("ctx", "head", None)
    out = P("ctx", None, "head")
    return jax.shard_map(
        shards, mesh=mesh, in_specs=(spec,) * 4, out_specs=(out,) * 3, check_vma=False
    )
```

```python
import functools

import jax
import jax.numpy as jnp
from jax import lax
from jax.experimental import pallas as pl
from jax.experimental.pallas import tpu as pltpu
from jax.sharding import PartitionSpec as P

HD = 128
TILE = 256
F32 = jnp.float32
BF16 = jnp.bfloat16
PARAMS = pltpu.CompilerParams(vmem_limit_bytes=40 * 1024 * 1024)


def dot(a, b, contract):
    return lax.dot_general(a, b, ((contract[:1], contract[1:]), ((), ())), preferred_element_type=F32)


def in_hbm(arrays):
    return [pltpu.with_memory_space_constraint(value, pltpu.HBM) for value in arrays]


def cost(flops, count):
    return pl.CostEstimate(flops=flops, bytes_accessed=2 * count, transcendentals=0)


def target_of(me, step, parts):
    if parts & (parts - 1) == 0:
        return me ^ step
    return (me + step) % parts


def source_of(me, step, parts):
    if parts & (parts - 1) == 0:
        return me ^ step
    return (me + parts - step) % parts


def steps_of(parts):
    return [0] + list(range(2, parts)) + [1]


def send(value, axis, target):
    count = lax.axis_size(axis)
    return lax.ppermute(value, axis, [(index, target(index)) for index in range(count)])


def copy_heads(inputs, parts, heads, step, head, count, target, at, sem):
    column = (target_of(lax.axis_index("head"), step, parts) * heads + head) * HD
    return [
        pltpu.make_async_copy(
            inputs[tensor].at[0, :, pl.ds(pl.multiple_of(column + index * HD, HD), HD)],
            target.at[at + 4 * index + tensor],
            sem,
        )
        for index in range(count)
        for tensor in range(4)
    ]


def first_kernel(parts, heads, count, late, *refs):
    inputs, outputs, (loaded, load_sem, copy_sem) = refs[:4], refs[4 : 3 + parts], refs[-3:]
    steps = range(1, parts)
    loads = [
        copy_heads(inputs, parts, heads, step, heads - late, late, loaded.at[step - 1], 0, load_sem.at[step - 1])
        for step in steps
    ]
    copies = [
        copy_heads(inputs, parts, heads, step, 0, count, outputs[step - 1], 0, copy_sem.at[step - 1])
        for step in steps
    ]
    for copy in sum(loads, []) + sum(copies, []):
        copy.start()
    for step in steps:
        for copy in loads[step - 1]:
            copy.wait()
        for index in range(late):
            query, keys, values, grads = (loaded[step - 1, 4 * index + tensor] for tensor in range(4))
            at = 4 * count + 2 * index
            outputs[step - 1][at] = dot(values, keys, (0, 0)).astype(BF16)
            outputs[step - 1][at + 1] = dot(query, grads, (0, 0)).astype(BF16)
    for copy in sum(copies, []):
        copy.wait()


@jax.named_scope("pack")
def pack_first(arrays, parts, heads, count, late):
    _, rows, full = arrays[0].shape
    units = 4 * count + 2 * late
    return pl.pallas_call(
        functools.partial(first_kernel, parts, heads, count, late),
        in_specs=[pl.BlockSpec(memory_space=pltpu.HBM)] * 4,
        out_specs=[pl.BlockSpec(memory_space=pltpu.VMEM)] * (parts - 1),
        out_shape=[jax.ShapeDtypeStruct((units, rows, HD), BF16)] * (parts - 1),
        scratch_shapes=[
            pltpu.VMEM((parts - 1, 4 * late, rows, HD), BF16),
            pltpu.SemaphoreType.DMA((parts - 1,)),
            pltpu.SemaphoreType.DMA((parts - 1,)),
        ],
        compiler_params=PARAMS,
        cost_estimate=cost(1000, 1024),
    )(*in_hbm(arrays))


def rest_kernel(parts, heads, chunks, *refs):
    inputs, outputs, (loaded, load_sem, copy_sem) = refs[:4], refs[4:-3], refs[-3:]
    late = chunks[-1]
    loads = copy_heads(inputs, parts, heads, 0, heads - late, late, loaded, 0, load_sem)
    copies, head = [], 0
    for chunk, count in enumerate(chunks):
        for step in range(parts):
            if chunk or not step:
                target = outputs[0] if not chunk else outputs[1 + (chunk - 1) * parts + step]
                copies += copy_heads(inputs, parts, heads, step, head, count, target, 0, copy_sem)
        head += count
    for copy in loads + copies:
        copy.start()
    for copy in loads:
        copy.wait()
    for index in range(late):
        query, keys, values, grads = (loaded[4 * index + tensor] for tensor in range(4))
        at = 4 * chunks[0] + 2 * index
        outputs[0][at] = dot(values, keys, (0, 0)).astype(BF16)
        outputs[0][at + 1] = dot(query, grads, (0, 0)).astype(BF16)
    for copy in copies:
        copy.wait()


@jax.named_scope("pack")
def pack_rest(arrays, parts, heads, chunks):
    _, rows, full = arrays[0].shape
    units = [4 * chunks[0] + 2 * chunks[-1]] + [4 * count for count in chunks[1:] for _ in range(parts)]
    flat = pl.pallas_call(
        functools.partial(rest_kernel, parts, heads, chunks),
        in_specs=[pl.BlockSpec(memory_space=pltpu.HBM)] * 4,
        out_specs=[pl.BlockSpec(memory_space=pltpu.VMEM)] * len(units),
        out_shape=[jax.ShapeDtypeStruct((unit, rows, HD), BF16) for unit in units],
        scratch_shapes=[
            pltpu.VMEM((4 * chunks[-1], rows, HD), BF16),
            pltpu.SemaphoreType.DMA,
            pltpu.SemaphoreType.DMA,
        ],
        compiler_params=PARAMS,
        cost_estimate=cost(1000, 1024),
    )(*in_hbm(arrays))
    return flat[0], [flat[1 + chunk * parts : 1 + (chunk + 1) * parts] for chunk in range(len(chunks) - 1)]


def state_kernel(parts, heads, extra, *refs):
    inputs, (out, give) = refs[:parts], refs[-2:]
    first = lax.axis_index("ctx") % 2 == 0
    half = HD // 2

    def share(head):
        for state in range(2):
            value = out[state, head]
            give[state, head] = jnp.where(first, value[half:], value[:half]).astype(BF16)

    for head in range(heads):
        query, keys, values, grads = (
            jnp.concatenate([ref[4 * head + tensor] for ref in inputs], 0) for tensor in range(4)
        )
        out[0, head] = dot(values, keys, (0, 0))
        out[1, head] = dot(query, grads, (0, 0))
        share(head)
    for late in range(extra):
        for state in range(2):
            at = 4 * heads + 2 * late + state
            out[state, heads + late] = sum(ref[at].astype(F32) for ref in inputs)
        share(heads + late)


@jax.named_scope("own_states")
def own_states(received, heads, extra, before):
    parts = len(received)
    rows = received[0].shape[1]
    return pl.pallas_call(
        functools.partial(state_kernel, parts, heads, extra),
        in_specs=[pl.BlockSpec(memory_space=pltpu.VMEM)] * parts
        + [pl.BlockSpec(memory_space=pl.ANY)] * len(before),
        out_shape=[
            jax.ShapeDtypeStruct((2, heads + extra, HD, HD), F32),
            jax.ShapeDtypeStruct((2, heads + extra, HD // 2, HD), BF16),
        ],
        compiler_params=PARAMS,
        cost_estimate=cost(1000, 1024),
    )(*received, *before)


def pick_kernel(chips, steps, own, partner, *refs):
    outputs = refs[-len(steps) :]
    me = lax.axis_index("ctx")
    chip, core = me // 2, me % 2
    half = HD // 2
    at = pl.ds(pl.multiple_of(core * half, half), half)
    keys, query = ((own[state, :, at] + partner[state].astype(F32)).astype(BF16) for state in range(2))
    for step, out in zip(steps, outputs):
        out[...] = jnp.where(chip + step < chips, keys, query)


@jax.named_scope("chip_states")
def chip_states(own, partner, chips, steps, before=()):
    _, heads, rows, _ = own.shape
    return pl.pallas_call(
        functools.partial(pick_kernel, chips, steps),
        in_specs=[pl.BlockSpec(memory_space=pltpu.VMEM)] * 2
        + [pl.BlockSpec(memory_space=pl.ANY)] * len(before),
        out_shape=[jax.ShapeDtypeStruct((heads, rows // 2, HD), BF16)] * len(steps),
        compiler_params=PARAMS,
        cost_estimate=cost(1000, 1024),
    )(own, partner, *before)


def finish_kernel(chips, own, partner, *refs):
    others, (mine, give) = refs[:-2], refs[-2:]
    me = lax.axis_index("ctx")
    chip, core = me // 2, me % 2
    half = HD // 2
    at = pl.ds(pl.multiple_of(core * half, half), half)
    keys = query = jnp.zeros(others[0].shape, F32)
    for step, ref in enumerate(others, 1):
        part = ref[...].astype(F32)
        keys = keys + jnp.where(chip >= step, part, 0.0)
        query = query + jnp.where(chip < step, part, 0.0)
    mine[0] = (keys + jnp.where(core == 1, partner[0].astype(F32), 0.0)).astype(BF16)
    mine[1] = (query + jnp.where(core == 0, partner[1].astype(F32), 0.0)).astype(BF16)
    give[0] = (keys + jnp.where(core == 0, own[0, :, at], 0.0)).astype(BF16)
    give[1] = (query + jnp.where(core == 1, own[1, :, at], 0.0)).astype(BF16)


@jax.named_scope("chip_states")
def finished(own, partner, others):
    _, heads, rows, _ = own.shape
    return pl.pallas_call(
        functools.partial(finish_kernel, len(others) + 1),
        out_shape=[jax.ShapeDtypeStruct((2, heads, rows // 2, HD), BF16)] * 2,
        compiler_params=PARAMS,
        cost_estimate=cost(1000, 1024),
    )(own, partner, *others)


def exchanged(own, give, *before):
    spans = lax.axis_size("ctx")
    chips = spans // 2
    partner = send(give, "ctx", lambda index: index ^ 1)
    others = []
    for first in range(1, chips, 2):
        steps = list(range(first, min(first + 2, chips)))
        for step, value in zip(steps, chip_states(own, partner, chips, steps, others[-2:][:1] + list(before if others else ()))):
            others.append(send(value, "ctx", lambda index: (index + 2 * step) % spans))
    mine, half = finished(own, partner, others)
    return mine, send(half, "ctx", lambda index: index ^ 1)


def read_states(refs, head):
    first = lax.axis_index("ctx") % 2 == 0
    mine, theirs = refs
    return (
        jnp.concatenate(
            [
                jnp.where(first, mine[state, head], theirs[state, head]),
                jnp.where(first, theirs[state, head], mine[state, head]),
            ],
            0,
        )
        for state in range(2)
    )


def grads_kernel(parts, factor, groups, *refs):
    outputs, token, (ordered, staged, sem) = refs[-7:-4], refs[-4], refs[-3:]
    me = lax.axis_index("head")
    rows = refs[0].shape[1]
    length = parts * rows
    tiles = length // TILE
    row = lax.broadcasted_iota(jnp.int32, (TILE, TILE), 0)
    column = lax.broadcasted_iota(jnp.int32, (TILE, TILE), 1)
    low, high = column <= row, row <= column

    def scores(a, b, keep):
        value = dot(a, b, (1, 1))
        if keep is not None:
            value = jnp.where(keep, value, 0.0)
        return value.astype(BF16)

    def total(lefts, rights):
        value = dot(jnp.concatenate(lefts, 1), jnp.concatenate(rights, 0), (1, 0))
        return (value * factor).astype(BF16)

    copies = []

    def store(slot, column, index, tile, value):
        at = pl.ds(tile * TILE, TILE)
        staged[slot, index, at] = value
        copies.append(
            pltpu.make_async_copy(
                staged.at[slot, index, at],
                outputs[index].at[0, at, pl.ds(column * HD, HD)],
                sem.at[slot, index, tile],
            )
        )
        copies[-1].start()

    slot = 0
    for group, (offset, first, heads) in enumerate(groups):
        arrays = refs[group * (parts + 2) :][: parts + 2]
        received, states = arrays[:parts], arrays[parts:]
        for head in range(heads):
            for step, ref in zip(steps_of(parts), received):
                place = source_of(me, step, parts)
                for tensor in range(4):
                    ordered[slot, tensor, place] = ref[4 * head + tensor]
            key_state, query_state = read_states(states, head + offset)
            query_turned = query_state.astype(F32).T.astype(BF16)
            query, keys, values, grads = (
                ordered[slot, tensor].reshape(tiles, TILE, HD) for tensor in range(4)
            )
            for i in range(tiles):
                before, after = range(i + 1), range(i, tiles)
                column = first + head
                store(slot, column, 0, i, total(
                    [scores(grads[i], values[j], low if i == j else None) for j in before] + [grads[i]],
                    [keys[j] for j in before] + [key_state],
                ))
                store(slot, column, 1, i, total(
                    [scores(values[i], grads[j], high if i == j else None) for j in after] + [values[i]],
                    [query[j] for j in after] + [query_turned],
                ))
                store(slot, column, 2, i, total(
                    [scores(keys[i], query[j], high if i == j else None) for j in after] + [keys[i]],
                    [grads[j] for j in after] + [query_state],
                ))
            slot += 1
    for copy in copies:
        copy.wait()
    token[...] = jnp.zeros_like(token)


@jax.named_scope("gradients")
def gradients(groups, held, group, factor):
    parts = len(groups[0][0])
    rows = groups[0][0][0].shape[1]
    length = parts * rows
    heads = sum(item[-1] for item in groups)
    arrays = [value for received, states, *_ in groups for value in (*received, *states)]
    return pl.pallas_call(
        functools.partial(grads_kernel, parts, factor, [item[2:] for item in groups]),
        in_specs=[pl.BlockSpec(memory_space=pltpu.VMEM)] * len(arrays)
        + [pl.BlockSpec(memory_space=pltpu.HBM)] * len(held),
        out_specs=[pl.BlockSpec(memory_space=pltpu.HBM)] * 3 + [pl.BlockSpec(memory_space=pltpu.VMEM)],
        out_shape=[jax.ShapeDtypeStruct((1, length, group), BF16)] * 3
        + [jax.ShapeDtypeStruct((8, HD), F32)],
        scratch_shapes=[
            pltpu.VMEM((heads, 4, parts, rows, HD), BF16),
            pltpu.VMEM((heads, 3, length, HD), BF16),
            pltpu.SemaphoreType.DMA((heads, 3, length // TILE)),
        ],
        input_output_aliases={len(arrays) + index: index for index in range(len(held))},
        compiler_params=PARAMS,
        cost_estimate=cost(1000, 1024),
    )(*arrays, *held)


def shards(query, keys, values, grad_out):
    parts = lax.axis_size("head")
    spans = lax.axis_size("ctx")
    _, rows, full = query.shape
    group = full // parts
    heads = group // HD
    factor = (HD * rows * parts * spans) ** -0.5
    late = max(1, heads // 4)
    middle = (heads - late) // 2
    chunks = [heads - late - middle, middle, late]
    arrays = (query, keys, values, grad_out)
    first = pack_first(arrays, parts, heads, chunks[0], late)
    own, packed = pack_rest(arrays, parts, heads, chunks)

    def exchange(own, values):
        return [own] + [
            send(values[step - 1], "head", lambda index: target_of(index, step, parts))
            for step in steps_of(parts)[1:]
        ]

    received = [exchange(own, first)] + [exchange(values[0], values[1:]) for values in packed]
    early = exchanged(*own_states(received[0], chunks[0], late, []))
    *held, token = gradients([(received[0], early, 0, 0, chunks[0])], (), group, factor)
    second = exchanged(*own_states(received[1], middle, 0, [early[0]]), token)
    *held, _ = gradients(
        [
            (received[2], early, chunks[0], heads - late, late),
            (received[1], second, 0, chunks[0], middle),
        ],
        held,
        group,
        factor,
    )
    return tuple(held)


def solution(mesh):
    spec = P("ctx", "head", None)
    out = P("ctx", None, "head")
    return jax.shard_map(
        shards, mesh=mesh, in_specs=(spec,) * 4, out_specs=(out,) * 3, check_vma=False
    )
```

```python
import functools

import jax
import jax.numpy as jnp
from jax import lax
from jax.experimental import pallas as pl
from jax.experimental.pallas import tpu as pltpu
from jax.sharding import PartitionSpec as P

HD = 128
TILE = 256
F32 = jnp.float32
BF16 = jnp.bfloat16
PARAMS = pltpu.CompilerParams(vmem_limit_bytes=40 * 1024 * 1024)


def dot(a, b, contract):
    return lax.dot_general(a, b, ((contract[:1], contract[1:]), ((), ())), preferred_element_type=F32)


def in_hbm(arrays):
    return [pltpu.with_memory_space_constraint(value, pltpu.HBM) for value in arrays]


def cost(flops, count):
    return pl.CostEstimate(flops=flops, bytes_accessed=2 * count, transcendentals=0)


def target_of(me, step, parts):
    if parts & (parts - 1) == 0:
        return me ^ step
    return (me + step) % parts


def source_of(me, step, parts):
    if parts & (parts - 1) == 0:
        return me ^ step
    return (me + parts - step) % parts


def steps_of(parts):
    return [0] + list(range(2, parts)) + [1]


def send(value, axis, target):
    count = lax.axis_size(axis)
    return lax.ppermute(value, axis, [(index, target(index)) for index in range(count)])


def copy_heads(inputs, parts, heads, step, head, count, target, at, sem):
    column = (target_of(lax.axis_index("head"), step, parts) * heads + head) * HD
    return [
        pltpu.make_async_copy(
            inputs[tensor].at[0, :, pl.ds(pl.multiple_of(column + index * HD, HD), HD)],
            target.at[at + 4 * index + tensor],
            sem,
        )
        for index in range(count)
        for tensor in range(4)
    ]


def first_kernel(parts, heads, count, late, *refs):
    inputs, outputs, (loaded, load_sem, copy_sem) = refs[:4], refs[4 : 3 + parts], refs[-3:]
    steps = range(1, parts)
    loads = [
        copy_heads(inputs, parts, heads, step, heads - late, late, loaded.at[step - 1], 0, load_sem.at[step - 1])
        for step in steps
    ]
    copies = [
        copy_heads(inputs, parts, heads, step, 0, count, outputs[step - 1], 0, copy_sem.at[step - 1])
        for step in steps
    ]
    for copy in sum(loads, []) + sum(copies, []):
        copy.start()
    for step in steps:
        for copy in loads[step - 1]:
            copy.wait()
        for index in range(late):
            query, keys, values, grads = (loaded[step - 1, 4 * index + tensor] for tensor in range(4))
            at = 4 * count + 2 * index
            outputs[step - 1][at] = dot(values, keys, (0, 0)).astype(BF16)
            outputs[step - 1][at + 1] = dot(query, grads, (0, 0)).astype(BF16)
    for copy in sum(copies, []):
        copy.wait()


@jax.named_scope("pack")
def pack_first(arrays, parts, heads, count, late):
    _, rows, full = arrays[0].shape
    units = 4 * count + 2 * late
    return pl.pallas_call(
        functools.partial(first_kernel, parts, heads, count, late),
        in_specs=[pl.BlockSpec(memory_space=pltpu.HBM)] * 4,
        out_specs=[pl.BlockSpec(memory_space=pltpu.VMEM)] * (parts - 1),
        out_shape=[jax.ShapeDtypeStruct((units, rows, HD), BF16)] * (parts - 1),
        scratch_shapes=[
            pltpu.VMEM((parts - 1, 4 * late, rows, HD), BF16),
            pltpu.SemaphoreType.DMA((parts - 1,)),
            pltpu.SemaphoreType.DMA((parts - 1,)),
        ],
        compiler_params=PARAMS,
        cost_estimate=cost(1000, 1024),
    )(*in_hbm(arrays))


def rest_kernel(parts, heads, chunks, *refs):
    inputs, outputs, (loaded, load_sem, copy_sem) = refs[:4], refs[4:-3], refs[-3:]
    late = chunks[-1]
    loads = copy_heads(inputs, parts, heads, 0, heads - late, late, loaded, 0, load_sem)
    copies, head = [], 0
    for chunk, count in enumerate(chunks):
        for step in range(parts):
            if chunk or not step:
                target = outputs[0] if not chunk else outputs[1 + (chunk - 1) * parts + step]
                copies += copy_heads(inputs, parts, heads, step, head, count, target, 0, copy_sem)
        head += count
    for copy in loads + copies:
        copy.start()
    for copy in loads:
        copy.wait()
    for index in range(late):
        query, keys, values, grads = (loaded[4 * index + tensor] for tensor in range(4))
        at = 4 * chunks[0] + 2 * index
        outputs[0][at] = dot(values, keys, (0, 0)).astype(BF16)
        outputs[0][at + 1] = dot(query, grads, (0, 0)).astype(BF16)
    for copy in copies:
        copy.wait()


@jax.named_scope("pack")
def pack_rest(arrays, parts, heads, chunks):
    _, rows, full = arrays[0].shape
    units = [4 * chunks[0] + 2 * chunks[-1]] + [4 * count for count in chunks[1:] for _ in range(parts)]
    flat = pl.pallas_call(
        functools.partial(rest_kernel, parts, heads, chunks),
        in_specs=[pl.BlockSpec(memory_space=pltpu.HBM)] * 4,
        out_specs=[pl.BlockSpec(memory_space=pltpu.VMEM)] * len(units),
        out_shape=[jax.ShapeDtypeStruct((unit, rows, HD), BF16) for unit in units],
        scratch_shapes=[
            pltpu.VMEM((4 * chunks[-1], rows, HD), BF16),
            pltpu.SemaphoreType.DMA,
            pltpu.SemaphoreType.DMA,
        ],
        compiler_params=PARAMS,
        cost_estimate=cost(1000, 1024),
    )(*in_hbm(arrays))
    return flat[0], [flat[1 + chunk * parts : 1 + (chunk + 1) * parts] for chunk in range(len(chunks) - 1)]


def state_kernel(parts, heads, extra, *refs):
    inputs, (out, give) = refs[:parts], refs[-2:]
    first = lax.axis_index("ctx") % 2 == 0
    half = HD // 2

    def share(head):
        for state in range(2):
            value = out[state, head]
            give[state, head] = jnp.where(first, value[half:], value[:half]).astype(BF16)

    for head in range(heads):
        query, keys, values, grads = (
            jnp.concatenate([ref[4 * head + tensor] for ref in inputs], 0) for tensor in range(4)
        )
        out[0, head] = dot(values, keys, (0, 0))
        out[1, head] = dot(query, grads, (0, 0))
        share(head)
    for late in range(extra):
        for state in range(2):
            at = 4 * heads + 2 * late + state
            out[state, heads + late] = sum(ref[at].astype(F32) for ref in inputs)
        share(heads + late)


@jax.named_scope("own_states")
def own_states(received, heads, extra, before):
    parts = len(received)
    rows = received[0].shape[1]
    return pl.pallas_call(
        functools.partial(state_kernel, parts, heads, extra),
        in_specs=[pl.BlockSpec(memory_space=pltpu.VMEM)] * parts
        + [pl.BlockSpec(memory_space=pl.ANY)] * len(before),
        out_shape=[
            jax.ShapeDtypeStruct((2, heads + extra, HD, HD), F32),
            jax.ShapeDtypeStruct((2, heads + extra, HD // 2, HD), BF16),
        ],
        compiler_params=PARAMS,
        cost_estimate=cost(1000, 1024),
    )(*received, *before)


def pick_kernel(chips, steps, own, partner, *refs):
    outputs = refs[-len(steps) :]
    me = lax.axis_index("ctx")
    chip, core = me // 2, me % 2
    half = HD // 2
    at = pl.ds(pl.multiple_of(core * half, half), half)
    keys, query = ((own[state, :, at] + partner[state].astype(F32)).astype(BF16) for state in range(2))
    for step, out in zip(steps, outputs):
        out[...] = jnp.where(chip + step < chips, keys, query)


@jax.named_scope("chip_states")
def chip_states(own, partner, chips, steps, before=()):
    _, heads, rows, _ = own.shape
    return pl.pallas_call(
        functools.partial(pick_kernel, chips, steps),
        in_specs=[pl.BlockSpec(memory_space=pltpu.VMEM)] * 2
        + [pl.BlockSpec(memory_space=pl.ANY)] * len(before),
        out_shape=[jax.ShapeDtypeStruct((heads, rows // 2, HD), BF16)] * len(steps),
        compiler_params=PARAMS,
        cost_estimate=cost(1000, 1024),
    )(own, partner, *before)


def finish_kernel(chips, own, partner, *refs):
    others, (mine, give) = refs[: chips - 1], refs[-2:]
    me = lax.axis_index("ctx")
    chip, core = me // 2, me % 2
    half = HD // 2
    at = pl.ds(pl.multiple_of(core * half, half), half)
    keys = query = jnp.zeros(others[0].shape, F32)
    for step, ref in enumerate(others, 1):
        part = ref[...].astype(F32)
        keys = keys + jnp.where(chip >= step, part, 0.0)
        query = query + jnp.where(chip < step, part, 0.0)
    mine[0] = (keys + jnp.where(core == 1, partner[0].astype(F32), 0.0)).astype(BF16)
    mine[1] = (query + jnp.where(core == 0, partner[1].astype(F32), 0.0)).astype(BF16)
    give[0] = (keys + jnp.where(core == 0, own[0, :, at], 0.0)).astype(BF16)
    give[1] = (query + jnp.where(core == 1, own[1, :, at], 0.0)).astype(BF16)


@jax.named_scope("chip_states")
def finished(own, partner, others, before):
    _, heads, rows, _ = own.shape
    return pl.pallas_call(
        functools.partial(finish_kernel, len(others) + 1),
        in_specs=[pl.BlockSpec(memory_space=pltpu.VMEM)] * (2 + len(others))
        + [pl.BlockSpec(memory_space=pl.ANY)] * len(before),
        out_shape=[jax.ShapeDtypeStruct((2, heads, rows // 2, HD), BF16)] * 2,
        compiler_params=PARAMS,
        cost_estimate=cost(1000, 1024),
    )(own, partner, *others, *before)


def exchanged(own, give, before=(), last=()):
    spans = lax.axis_size("ctx")
    chips = spans // 2
    partner = send(give, "ctx", lambda index: index ^ 1)
    others = []
    for first in range(1, chips, 2):
        steps = list(range(first, min(first + 2, chips)))
        for step, value in zip(steps, chip_states(own, partner, chips, steps, others[-2:][:1] + list(before if others else ()))):
            others.append(send(value, "ctx", lambda index: (index + 2 * step) % spans))
    mine, half = finished(own, partner, others, last)
    return mine, send(half, "ctx", lambda index: index ^ 1)


def read_states(refs, head):
    first = lax.axis_index("ctx") % 2 == 0
    mine, theirs = refs
    return (
        jnp.concatenate(
            [
                jnp.where(first, mine[state, head], theirs[state, head]),
                jnp.where(first, theirs[state, head], mine[state, head]),
            ],
            0,
        )
        for state in range(2)
    )


def grads_kernel(parts, factor, groups, *refs):
    outputs, token, (ordered, staged, sem) = refs[-7:-4], refs[-4], refs[-3:]
    me = lax.axis_index("head")
    rows = refs[0].shape[1]
    length = parts * rows
    tiles = length // TILE
    row = lax.broadcasted_iota(jnp.int32, (TILE, TILE), 0)
    column = lax.broadcasted_iota(jnp.int32, (TILE, TILE), 1)
    low, high = column <= row, row <= column

    def scores(a, b, keep):
        value = dot(a, b, (1, 1))
        if keep is not None:
            value = jnp.where(keep, value, 0.0)
        return value.astype(BF16)

    def total(lefts, rights):
        value = dot(jnp.concatenate(lefts, 1), jnp.concatenate(rights, 0), (1, 0))
        return (value * factor).astype(BF16)

    copies = []

    def store(slot, column, index, tile, value):
        at = pl.ds(tile * TILE, TILE)
        staged[slot, index, at] = value
        copies.append(
            pltpu.make_async_copy(
                staged.at[slot, index, at],
                outputs[index].at[0, at, pl.ds(column * HD, HD)],
                sem.at[slot, index, tile],
            )
        )
        copies[-1].start()

    slot = 0
    for group, (offset, first, heads) in enumerate(groups):
        arrays = refs[group * (parts + 2) :][: parts + 2]
        received, states = arrays[:parts], arrays[parts:]
        for head in range(heads):
            for step, ref in zip(steps_of(parts), received):
                place = source_of(me, step, parts)
                for tensor in range(4):
                    ordered[slot, tensor, place] = ref[4 * head + tensor]
            key_state, query_state = read_states(states, head + offset)
            query_turned = query_state.astype(F32).T.astype(BF16)
            query, keys, values, grads = (
                ordered[slot, tensor].reshape(tiles, TILE, HD) for tensor in range(4)
            )
            for i in range(tiles):
                before, after = range(i + 1), range(i, tiles)
                column = first + head
                store(slot, column, 0, i, total(
                    [scores(grads[i], values[j], low if i == j else None) for j in before] + [grads[i]],
                    [keys[j] for j in before] + [key_state],
                ))
                store(slot, column, 1, i, total(
                    [scores(values[i], grads[j], high if i == j else None) for j in after] + [values[i]],
                    [query[j] for j in after] + [query_turned],
                ))
                store(slot, column, 2, i, total(
                    [scores(keys[i], query[j], high if i == j else None) for j in after] + [keys[i]],
                    [grads[j] for j in after] + [query_state],
                ))
            slot += 1
    for copy in copies:
        copy.wait()
    token[...] = jnp.zeros_like(token)


@jax.named_scope("gradients")
def gradients(groups, held, group, factor):
    parts = len(groups[0][0])
    rows = groups[0][0][0].shape[1]
    length = parts * rows
    heads = sum(item[-1] for item in groups)
    arrays = [value for received, states, *_ in groups for value in (*received, *states)]
    return pl.pallas_call(
        functools.partial(grads_kernel, parts, factor, [item[2:] for item in groups]),
        in_specs=[pl.BlockSpec(memory_space=pltpu.VMEM)] * len(arrays)
        + [pl.BlockSpec(memory_space=pltpu.HBM)] * len(held),
        out_specs=[pl.BlockSpec(memory_space=pltpu.HBM)] * 3 + [pl.BlockSpec(memory_space=pltpu.VMEM)],
        out_shape=[jax.ShapeDtypeStruct((1, length, group), BF16)] * 3
        + [jax.ShapeDtypeStruct((8, HD), F32)],
        scratch_shapes=[
            pltpu.VMEM((heads, 4, parts, rows, HD), BF16),
            pltpu.VMEM((heads, 3, length, HD), BF16),
            pltpu.SemaphoreType.DMA((heads, 3, length // TILE)),
        ],
        input_output_aliases={len(arrays) + index: index for index in range(len(held))},
        compiler_params=PARAMS,
        cost_estimate=cost(1000, 1024),
    )(*arrays, *held)


def shards(query, keys, values, grad_out):
    parts = lax.axis_size("head")
    spans = lax.axis_size("ctx")
    _, rows, full = query.shape
    group = full // parts
    heads = group // HD
    factor = (HD * rows * parts * spans) ** -0.5
    late = max(1, heads // 4)
    middle = (heads - late) // 2
    chunks = [heads - late - middle, middle, late]
    arrays = (query, keys, values, grad_out)
    first = pack_first(arrays, parts, heads, chunks[0], late)
    own, packed = pack_rest(arrays, parts, heads, chunks)

    def exchange(own, values):
        return [own] + [
            send(values[step - 1], "head", lambda index: target_of(index, step, parts))
            for step in steps_of(parts)[1:]
        ]

    received = [exchange(own, first)] + [exchange(values[0], values[1:]) for values in packed]
    early = exchanged(*own_states(received[0], chunks[0], late, []))
    *held, token = gradients([(received[0], early, 0, 0, chunks[0])], (), group, factor)
    second = exchanged(*own_states(received[1], middle, 0, [early[0]]), [token], received[2][1:])
    *held, _ = gradients(
        [
            (received[2], early, chunks[0], heads - late, late),
            (received[1], second, 0, chunks[0], middle),
        ],
        held,
        group,
        factor,
    )
    return tuple(held)


def solution(mesh):
    spec = P("ctx", "head", None)
    out = P("ctx", None, "head")
    return jax.shard_map(
        shards, mesh=mesh, in_specs=(spec,) * 4, out_specs=(out,) * 3, check_vma=False
    )
```

```python
import functools

import jax
import jax.numpy as jnp
from jax import lax
from jax.experimental import pallas as pl
from jax.experimental.pallas import tpu as pltpu
from jax.sharding import PartitionSpec as P

HD = 128
TILE = 256
F32 = jnp.float32
BF16 = jnp.bfloat16
PARAMS = pltpu.CompilerParams(vmem_limit_bytes=40 * 1024 * 1024)


def dot(a, b, contract):
    return lax.dot_general(a, b, ((contract[:1], contract[1:]), ((), ())), preferred_element_type=F32)


def in_hbm(arrays):
    return [pltpu.with_memory_space_constraint(value, pltpu.HBM) for value in arrays]


def cost(flops, count):
    return pl.CostEstimate(flops=flops, bytes_accessed=2 * count, transcendentals=0)


def target_of(me, step, parts):
    if parts & (parts - 1) == 0:
        return me ^ step
    return (me + step) % parts


def source_of(me, step, parts):
    if parts & (parts - 1) == 0:
        return me ^ step
    return (me + parts - step) % parts


def steps_of(parts):
    return [0] + list(range(2, parts)) + [1]


def send(value, axis, target):
    count = lax.axis_size(axis)
    return lax.ppermute(value, axis, [(index, target(index)) for index in range(count)])


def copy_heads(inputs, parts, heads, step, head, count, target, at, sem):
    column = (target_of(lax.axis_index("head"), step, parts) * heads + head) * HD
    return [
        pltpu.make_async_copy(
            inputs[tensor].at[0, :, pl.ds(pl.multiple_of(column + index * HD, HD), HD)],
            target.at[at + 4 * index + tensor],
            sem,
        )
        for index in range(count)
        for tensor in range(4)
    ]


def first_kernel(parts, heads, count, late, *refs):
    inputs, outputs, (loaded, load_sem, copy_sem) = refs[:4], refs[4 : 3 + parts], refs[-3:]
    steps = range(1, parts)
    loads = [
        copy_heads(inputs, parts, heads, step, heads - late, late, loaded.at[step - 1], 0, load_sem.at[step - 1])
        for step in steps
    ]
    copies = [
        copy_heads(inputs, parts, heads, step, 0, count, outputs[step - 1], 0, copy_sem.at[step - 1])
        for step in steps
    ]
    for copy in sum(loads, []) + sum(copies, []):
        copy.start()
    for step in steps:
        for copy in loads[step - 1]:
            copy.wait()
        for index in range(late):
            query, keys, values, grads = (loaded[step - 1, 4 * index + tensor] for tensor in range(4))
            at = 4 * count + 2 * index
            outputs[step - 1][at] = dot(values, keys, (0, 0)).astype(BF16)
            outputs[step - 1][at + 1] = dot(query, grads, (0, 0)).astype(BF16)
    for copy in sum(copies, []):
        copy.wait()


@jax.named_scope("pack")
def pack_first(arrays, parts, heads, count, late):
    _, rows, full = arrays[0].shape
    units = 4 * count + 2 * late
    return pl.pallas_call(
        functools.partial(first_kernel, parts, heads, count, late),
        in_specs=[pl.BlockSpec(memory_space=pltpu.HBM)] * 4,
        out_specs=[pl.BlockSpec(memory_space=pltpu.VMEM)] * (parts - 1),
        out_shape=[jax.ShapeDtypeStruct((units, rows, HD), BF16)] * (parts - 1),
        scratch_shapes=[
            pltpu.VMEM((parts - 1, 4 * late, rows, HD), BF16),
            pltpu.SemaphoreType.DMA((parts - 1,)),
            pltpu.SemaphoreType.DMA((parts - 1,)),
        ],
        compiler_params=PARAMS,
        cost_estimate=cost(1000, 1024),
    )(*in_hbm(arrays))


def rest_kernel(parts, heads, chunks, *refs):
    inputs, outputs, (loaded, load_sem, copy_sem) = refs[:4], refs[4:-3], refs[-3:]
    late = chunks[-1]
    loads = copy_heads(inputs, parts, heads, 0, heads - late, late, loaded, 0, load_sem)
    copies, head = [], 0
    for chunk, count in enumerate(chunks):
        for step in range(parts):
            if chunk or not step:
                target = outputs[0] if not chunk else outputs[1 + (chunk - 1) * parts + step]
                copies += copy_heads(inputs, parts, heads, step, head, count, target, 0, copy_sem)
        head += count
    for copy in loads + copies:
        copy.start()
    for copy in loads:
        copy.wait()
    for index in range(late):
        query, keys, values, grads = (loaded[4 * index + tensor] for tensor in range(4))
        at = 4 * chunks[0] + 2 * index
        outputs[0][at] = dot(values, keys, (0, 0)).astype(BF16)
        outputs[0][at + 1] = dot(query, grads, (0, 0)).astype(BF16)
    for copy in copies:
        copy.wait()


@jax.named_scope("pack")
def pack_rest(arrays, parts, heads, chunks):
    _, rows, full = arrays[0].shape
    units = [4 * chunks[0] + 2 * chunks[-1]] + [4 * count for count in chunks[1:] for _ in range(parts)]
    flat = pl.pallas_call(
        functools.partial(rest_kernel, parts, heads, chunks),
        in_specs=[pl.BlockSpec(memory_space=pltpu.HBM)] * 4,
        out_specs=[pl.BlockSpec(memory_space=pltpu.VMEM)] * len(units),
        out_shape=[jax.ShapeDtypeStruct((unit, rows, HD), BF16) for unit in units],
        scratch_shapes=[
            pltpu.VMEM((4 * chunks[-1], rows, HD), BF16),
            pltpu.SemaphoreType.DMA,
            pltpu.SemaphoreType.DMA,
        ],
        compiler_params=PARAMS,
        cost_estimate=cost(1000, 1024),
    )(*in_hbm(arrays))
    return flat[0], [flat[1 + chunk * parts : 1 + (chunk + 1) * parts] for chunk in range(len(chunks) - 1)]


def state_kernel(parts, heads, extra, *refs):
    inputs, (out, give) = refs[:parts], refs[-2:]
    first = lax.axis_index("ctx") % 2 == 0
    half = HD // 2

    def share(head):
        for state in range(2):
            value = out[state, head]
            give[state, head] = jnp.where(first, value[half:], value[:half]).astype(BF16)

    for head in range(heads):
        query, keys, values, grads = (
            jnp.concatenate([ref[4 * head + tensor] for ref in inputs], 0) for tensor in range(4)
        )
        out[0, head] = dot(values, keys, (0, 0))
        out[1, head] = dot(query, grads, (0, 0))
        share(head)
    for late in range(extra):
        for state in range(2):
            at = 4 * heads + 2 * late + state
            out[state, heads + late] = sum(ref[at].astype(F32) for ref in inputs)
        share(heads + late)


@jax.named_scope("own_states")
def own_states(received, heads, extra, before):
    parts = len(received)
    rows = received[0].shape[1]
    return pl.pallas_call(
        functools.partial(state_kernel, parts, heads, extra),
        in_specs=[pl.BlockSpec(memory_space=pltpu.VMEM)] * parts
        + [pl.BlockSpec(memory_space=pl.ANY)] * len(before),
        out_shape=[
            jax.ShapeDtypeStruct((2, heads + extra, HD, HD), F32),
            jax.ShapeDtypeStruct((2, heads + extra, HD // 2, HD), BF16),
        ],
        compiler_params=PARAMS,
        cost_estimate=cost(1000, 1024),
    )(*received, *before)


def pick_kernel(chips, steps, own, partner, *refs):
    outputs = refs[-len(steps) :]
    me = lax.axis_index("ctx")
    chip, core = me // 2, me % 2
    half = HD // 2
    at = pl.ds(pl.multiple_of(core * half, half), half)
    keys, query = ((own[state, :, at] + partner[state].astype(F32)).astype(BF16) for state in range(2))
    for step, out in zip(steps, outputs):
        out[...] = jnp.where(chip + step < chips, keys, query)


@jax.named_scope("chip_states")
def chip_states(own, partner, chips, steps, before=()):
    _, heads, rows, _ = own.shape
    return pl.pallas_call(
        functools.partial(pick_kernel, chips, steps),
        in_specs=[pl.BlockSpec(memory_space=pltpu.VMEM)] * 2
        + [pl.BlockSpec(memory_space=pl.ANY)] * len(before),
        out_shape=[jax.ShapeDtypeStruct((heads, rows // 2, HD), BF16)] * len(steps),
        compiler_params=PARAMS,
        cost_estimate=cost(1000, 1024),
    )(own, partner, *before)


def finish_kernel(chips, own, partner, *refs):
    others, (mine, give) = refs[: chips - 1], refs[-2:]
    me = lax.axis_index("ctx")
    chip, core = me // 2, me % 2
    half = HD // 2
    at = pl.ds(pl.multiple_of(core * half, half), half)
    keys = query = jnp.zeros(others[0].shape, F32)
    for step, ref in enumerate(others, 1):
        part = ref[...].astype(F32)
        keys = keys + jnp.where(chip >= step, part, 0.0)
        query = query + jnp.where(chip < step, part, 0.0)
    mine[0] = (keys + jnp.where(core == 1, partner[0].astype(F32), 0.0)).astype(BF16)
    mine[1] = (query + jnp.where(core == 0, partner[1].astype(F32), 0.0)).astype(BF16)
    give[0] = (keys + jnp.where(core == 0, own[0, :, at], 0.0)).astype(BF16)
    give[1] = (query + jnp.where(core == 1, own[1, :, at], 0.0)).astype(BF16)


@jax.named_scope("chip_states")
def finished(own, partner, others, before):
    _, heads, rows, _ = own.shape
    return pl.pallas_call(
        functools.partial(finish_kernel, len(others) + 1),
        in_specs=[pl.BlockSpec(memory_space=pltpu.VMEM)] * (2 + len(others))
        + [pl.BlockSpec(memory_space=pl.ANY)] * len(before),
        out_shape=[jax.ShapeDtypeStruct((2, heads, rows // 2, HD), BF16)] * 2,
        compiler_params=PARAMS,
        cost_estimate=cost(1000, 1024),
    )(own, partner, *others, *before)


def exchanged(own, give, before=(), last=()):
    spans = lax.axis_size("ctx")
    chips = spans // 2
    partner = send(give, "ctx", lambda index: index ^ 1)
    others = []
    for first in range(1, chips, 2):
        steps = list(range(first, min(first + 2, chips)))
        for step, value in zip(steps, chip_states(own, partner, chips, steps, others[-2:][:1] + list(before if others else ()))):
            others.append(send(value, "ctx", lambda index: (index + 2 * step) % spans))
    mine, half = finished(own, partner, others, last)
    return mine, send(half, "ctx", lambda index: index ^ 1)


def read_states(refs, head):
    first = lax.axis_index("ctx") % 2 == 0
    mine, theirs = refs
    return (
        jnp.concatenate(
            [
                jnp.where(first, mine[state, head], theirs[state, head]),
                jnp.where(first, theirs[state, head], mine[state, head]),
            ],
            0,
        )
        for state in range(2)
    )


def grads_kernel(parts, factor, groups, *refs):
    outputs, token, (ordered, staged, sem) = refs[-7:-4], refs[-4], refs[-3:]
    me = lax.axis_index("head")
    rows = refs[0].shape[1]
    length = parts * rows
    tiles = length // TILE
    row = lax.broadcasted_iota(jnp.int32, (TILE, TILE), 0)
    column = lax.broadcasted_iota(jnp.int32, (TILE, TILE), 1)
    low, high = column <= row, row <= column

    def scores(a, b, keep):
        value = dot(a, b, (1, 1))
        if keep is not None:
            value = jnp.where(keep, value, 0.0)
        return value.astype(BF16)

    def total(lefts, rights):
        value = dot(jnp.concatenate(lefts, 1), jnp.concatenate(rights, 0), (1, 0))
        return (value * factor).astype(BF16)

    copies = []

    def store(slot, column, index, tile, value):
        at = pl.ds(tile * TILE, TILE)
        staged[slot, index, at] = value
        copies.append(
            pltpu.make_async_copy(
                staged.at[slot, index, at],
                outputs[index].at[0, at, pl.ds(column * HD, HD)],
                sem.at[slot, index, tile],
            )
        )
        copies[-1].start()

    slot = 0
    for group, (offset, first, heads) in enumerate(groups):
        arrays = refs[group * (parts + 2) :][: parts + 2]
        received, states = arrays[:parts], arrays[parts:]
        for head in range(heads):
            for step, ref in zip(steps_of(parts), received):
                place = source_of(me, step, parts)
                for tensor in range(4):
                    ordered[slot, tensor, place] = ref[4 * head + tensor]
            key_state, query_state = read_states(states, head + offset)
            query_turned = query_state.astype(F32).T.astype(BF16)
            query, keys, values, grads = (
                ordered[slot, tensor].reshape(tiles, TILE, HD) for tensor in range(4)
            )
            for i in range(tiles):
                before, after = range(i + 1), range(i, tiles)
                column = first + head
                store(slot, column, 0, i, total(
                    [scores(grads[i], values[j], low if i == j else None) for j in before] + [grads[i]],
                    [keys[j] for j in before] + [key_state],
                ))
                store(slot, column, 1, i, total(
                    [scores(values[i], grads[j], high if i == j else None) for j in after] + [values[i]],
                    [query[j] for j in after] + [query_turned],
                ))
                store(slot, column, 2, i, total(
                    [scores(keys[i], query[j], high if i == j else None) for j in after] + [keys[i]],
                    [grads[j] for j in after] + [query_state],
                ))
            slot += 1
    for copy in copies:
        copy.wait()
    token[...] = jnp.zeros_like(token)


@jax.named_scope("gradients")
def gradients(groups, held, group, factor):
    parts = len(groups[0][0])
    rows = groups[0][0][0].shape[1]
    length = parts * rows
    heads = sum(item[-1] for item in groups)
    arrays = [value for received, states, *_ in groups for value in (*received, *states)]
    return pl.pallas_call(
        functools.partial(grads_kernel, parts, factor, [item[2:] for item in groups]),
        in_specs=[pl.BlockSpec(memory_space=pltpu.VMEM)] * len(arrays)
        + [pl.BlockSpec(memory_space=pltpu.HBM)] * len(held),
        out_specs=[pl.BlockSpec(memory_space=pltpu.HBM)] * 3 + [pl.BlockSpec(memory_space=pltpu.VMEM)],
        out_shape=[jax.ShapeDtypeStruct((1, length, group), BF16)] * 3
        + [jax.ShapeDtypeStruct((8, HD), F32)],
        scratch_shapes=[
            pltpu.VMEM((heads, 4, parts, rows, HD), BF16),
            pltpu.VMEM((heads, 3, length, HD), BF16),
            pltpu.SemaphoreType.DMA((heads, 3, length // TILE)),
        ],
        input_output_aliases={len(arrays) + index: index for index in range(len(held))},
        compiler_params=PARAMS,
        cost_estimate=cost(1000, 1024),
    )(*arrays, *held)


def shards(query, keys, values, grad_out):
    parts = lax.axis_size("head")
    spans = lax.axis_size("ctx")
    _, rows, full = query.shape
    group = full // parts
    heads = group // HD
    factor = (HD * rows * parts * spans) ** -0.5
    late = max(1, heads // 4)
    middle = (heads - late) // 2
    chunks = [heads - late - middle, middle, late]
    arrays = (query, keys, values, grad_out)
    first = pack_first(arrays, parts, heads, chunks[0], late)
    own, packed = pack_rest(arrays, parts, heads, chunks)

    def exchange(own, values):
        return [own] + [
            send(values[step - 1], "head", lambda index: target_of(index, step, parts))
            for step in steps_of(parts)[1:]
        ]

    received = [exchange(own, first)] + [exchange(values[0], values[1:]) for values in packed]
    early = exchanged(*own_states(received[0], chunks[0], late, []))
    *held, token = gradients([(received[0], early, 0, 0, chunks[0])], (), group, factor)
    *held, ready = gradients([(received[2], early, chunks[0], heads - late, late)], held, group, factor)
    second = exchanged(*own_states(received[1], middle, 0, [early[0]]), [token], [ready])
    *held, _ = gradients([(received[1], second, 0, chunks[0], middle)], held, group, factor)
    return tuple(held)


def solution(mesh):
    spec = P("ctx", "head", None)
    out = P("ctx", None, "head")
    return jax.shard_map(
        shards, mesh=mesh, in_specs=(spec,) * 4, out_specs=(out,) * 3, check_vma=False
    )
```

```python
import functools

import jax
import jax.numpy as jnp
from jax import lax
from jax.experimental import pallas as pl
from jax.experimental.pallas import tpu as pltpu
from jax.sharding import PartitionSpec as P

HD = 128
TILE = 256
F32 = jnp.float32
BF16 = jnp.bfloat16
PARAMS = pltpu.CompilerParams(vmem_limit_bytes=40 * 1024 * 1024)


def dot(a, b, contract):
    return lax.dot_general(a, b, ((contract[:1], contract[1:]), ((), ())), preferred_element_type=F32)


def in_hbm(arrays):
    return [pltpu.with_memory_space_constraint(value, pltpu.HBM) for value in arrays]


def cost(flops, count):
    return pl.CostEstimate(flops=flops, bytes_accessed=2 * count, transcendentals=0)


def target_of(me, step, parts):
    if parts & (parts - 1) == 0:
        return me ^ step
    return (me + step) % parts


def source_of(me, step, parts):
    if parts & (parts - 1) == 0:
        return me ^ step
    return (me + parts - step) % parts


def steps_of(parts):
    return [0] + list(range(2, parts)) + [1]


def send(value, axis, target):
    count = lax.axis_size(axis)
    return lax.ppermute(value, axis, [(index, target(index)) for index in range(count)])


def copy_heads(inputs, parts, heads, step, head, count, target, at, sem):
    column = (target_of(lax.axis_index("head"), step, parts) * heads + head) * HD
    return [
        pltpu.make_async_copy(
            inputs[tensor].at[0, :, pl.ds(pl.multiple_of(column + index * HD, HD), HD)],
            target.at[at + 4 * index + tensor],
            sem,
        )
        for index in range(count)
        for tensor in range(4)
    ]


def first_kernel(parts, heads, count, late, *refs):
    inputs, outputs, (loaded, load_sem, copy_sem) = refs[:4], refs[4 : 3 + parts], refs[-3:]
    steps = range(1, parts)
    loads = [
        copy_heads(inputs, parts, heads, step, heads - late, late, loaded.at[step - 1], 0, load_sem.at[step - 1])
        for step in steps
    ]
    copies = [
        copy_heads(inputs, parts, heads, step, 0, count, outputs[step - 1], 0, copy_sem.at[step - 1])
        for step in steps
    ]
    for copy in sum(loads, []) + sum(copies, []):
        copy.start()
    for step in steps:
        for copy in loads[step - 1]:
            copy.wait()
        for index in range(late):
            query, keys, values, grads = (loaded[step - 1, 4 * index + tensor] for tensor in range(4))
            at = 4 * count + 2 * index
            outputs[step - 1][at] = dot(values, keys, (0, 0)).astype(BF16)
            outputs[step - 1][at + 1] = dot(query, grads, (0, 0)).astype(BF16)
    for copy in sum(copies, []):
        copy.wait()


@jax.named_scope("pack")
def pack_first(arrays, parts, heads, count, late):
    _, rows, full = arrays[0].shape
    units = 4 * count + 2 * late
    return pl.pallas_call(
        functools.partial(first_kernel, parts, heads, count, late),
        in_specs=[pl.BlockSpec(memory_space=pltpu.HBM)] * 4,
        out_specs=[pl.BlockSpec(memory_space=pltpu.VMEM)] * (parts - 1),
        out_shape=[jax.ShapeDtypeStruct((units, rows, HD), BF16)] * (parts - 1),
        scratch_shapes=[
            pltpu.VMEM((parts - 1, 4 * late, rows, HD), BF16),
            pltpu.SemaphoreType.DMA((parts - 1,)),
            pltpu.SemaphoreType.DMA((parts - 1,)),
        ],
        compiler_params=PARAMS,
        cost_estimate=cost(1000, 1024),
    )(*in_hbm(arrays))


def rest_kernel(parts, heads, chunks, *refs):
    inputs, outputs, (loaded, load_sem, copy_sem) = refs[:4], refs[4:-3], refs[-3:]
    late = chunks[-1]
    loads = copy_heads(inputs, parts, heads, 0, heads - late, late, loaded, 0, load_sem)
    copies, head = [], 0
    for chunk, count in enumerate(chunks):
        for step in range(parts):
            if chunk or not step:
                target = outputs[0] if not chunk else outputs[1 + (chunk - 1) * parts + step]
                copies += copy_heads(inputs, parts, heads, step, head, count, target, 0, copy_sem)
        head += count
    for copy in loads + copies:
        copy.start()
    for copy in loads:
        copy.wait()
    for index in range(late):
        query, keys, values, grads = (loaded[4 * index + tensor] for tensor in range(4))
        at = 4 * chunks[0] + 2 * index
        outputs[0][at] = dot(values, keys, (0, 0)).astype(BF16)
        outputs[0][at + 1] = dot(query, grads, (0, 0)).astype(BF16)
    for copy in copies:
        copy.wait()


@jax.named_scope("pack")
def pack_rest(arrays, parts, heads, chunks):
    _, rows, full = arrays[0].shape
    units = [4 * chunks[0] + 2 * chunks[-1]] + [4 * count for count in chunks[1:] for _ in range(parts)]
    flat = pl.pallas_call(
        functools.partial(rest_kernel, parts, heads, chunks),
        in_specs=[pl.BlockSpec(memory_space=pltpu.HBM)] * 4,
        out_specs=[pl.BlockSpec(memory_space=pltpu.VMEM)] * len(units),
        out_shape=[jax.ShapeDtypeStruct((unit, rows, HD), BF16) for unit in units],
        scratch_shapes=[
            pltpu.VMEM((4 * chunks[-1], rows, HD), BF16),
            pltpu.SemaphoreType.DMA,
            pltpu.SemaphoreType.DMA,
        ],
        compiler_params=PARAMS,
        cost_estimate=cost(1000, 1024),
    )(*in_hbm(arrays))
    return flat[0], [flat[1 + chunk * parts : 1 + (chunk + 1) * parts] for chunk in range(len(chunks) - 1)]


def state_kernel(parts, heads, extra, *refs):
    inputs, (out, give) = refs[:parts], refs[-2:]
    first = lax.axis_index("ctx") % 2 == 0
    half = HD // 2

    def share(head):
        for state in range(2):
            value = out[state, head]
            give[state, head] = jnp.where(first, value[half:], value[:half]).astype(BF16)

    for head in range(heads):
        query, keys, values, grads = (
            jnp.concatenate([ref[4 * head + tensor] for ref in inputs], 0) for tensor in range(4)
        )
        out[0, head] = dot(values, keys, (0, 0))
        out[1, head] = dot(query, grads, (0, 0))
        share(head)
    for late in range(extra):
        for state in range(2):
            at = 4 * heads + 2 * late + state
            out[state, heads + late] = sum(ref[at].astype(F32) for ref in inputs)
        share(heads + late)


@jax.named_scope("own_states")
def own_states(received, heads, extra, before):
    parts = len(received)
    rows = received[0].shape[1]
    return pl.pallas_call(
        functools.partial(state_kernel, parts, heads, extra),
        in_specs=[pl.BlockSpec(memory_space=pltpu.VMEM)] * parts
        + [pl.BlockSpec(memory_space=pl.ANY)] * len(before),
        out_shape=[
            jax.ShapeDtypeStruct((2, heads + extra, HD, HD), F32),
            jax.ShapeDtypeStruct((2, heads + extra, HD // 2, HD), BF16),
        ],
        compiler_params=PARAMS,
        cost_estimate=cost(1000, 1024),
    )(*received, *before)


def own_half(own, state):
    half = HD // 2
    first = lax.axis_index("ctx") % 2 == 0
    return jnp.where(first, own[state, :, :half], own[state, :, half:])


def group_kernel(bit, final, arrived, own, partner, *refs):
    others, out = refs[:arrived], refs[-1]
    chip = lax.axis_index("ctx") // 2
    totals = [
        own_half(own, state) + partner[state].astype(F32) + sum(ref[state].astype(F32) for ref in others)
        for state in range(2)
    ]
    if final:
        out[...] = jnp.where(chip & bit == 0, *totals).astype(BF16)
    else:
        for state in range(2):
            out[state] = totals[state].astype(BF16)


@jax.named_scope("chip_states")
def group_states(own, partner, others, bit, final, before):
    arrays = (own, partner, *others)
    shape = partner.shape[1:] if final else partner.shape
    return pl.pallas_call(
        functools.partial(group_kernel, bit, final, len(others)),
        in_specs=[pl.BlockSpec(memory_space=pltpu.VMEM)] * len(arrays)
        + [pl.BlockSpec(memory_space=pl.ANY)] * len(before),
        out_shape=jax.ShapeDtypeStruct(shape, BF16),
        compiler_params=PARAMS,
        cost_estimate=cost(1000, 1024),
    )(*arrays, *before)


def finish_kernel(arrived, own, partner, *refs):
    others, (mine, give) = refs[:arrived], refs[-2:]
    me = lax.axis_index("ctx")
    chip, core = me // 2, me % 2
    keys = query = jnp.zeros(mine.shape[1:], F32)
    for step, ref in enumerate(others):
        upper = chip & (1 << step) != 0
        pair = (ref, ref) if step == arrived - 1 else (ref.at[0], ref.at[1])
        keys = keys + jnp.where(upper, pair[0][...].astype(F32), 0.0)
        query = query + jnp.where(upper, 0.0, pair[1][...].astype(F32))
    mine[0] = (keys + jnp.where(core == 1, partner[0].astype(F32), 0.0)).astype(BF16)
    mine[1] = (query + jnp.where(core == 0, partner[1].astype(F32), 0.0)).astype(BF16)
    give[0] = (keys + jnp.where(core == 0, own_half(own, 0), 0.0)).astype(BF16)
    give[1] = (query + jnp.where(core == 1, own_half(own, 1), 0.0)).astype(BF16)


@jax.named_scope("chip_states")
def finished(own, partner, others, before):
    return pl.pallas_call(
        functools.partial(finish_kernel, len(others)),
        in_specs=[pl.BlockSpec(memory_space=pltpu.VMEM)] * (2 + len(others))
        + [pl.BlockSpec(memory_space=pl.ANY)] * len(before),
        out_shape=[jax.ShapeDtypeStruct(partner.shape, BF16)] * 2,
        compiler_params=PARAMS,
        cost_estimate=cost(1000, 1024),
    )(own, partner, *others, *before)


def exchanged(own, give, before=(), last=()):
    chips = lax.axis_size("ctx") // 2
    assert chips & (chips - 1) == 0
    partner = send(give, "ctx", lambda index: index ^ 1)
    others, bit = [], 1
    while bit < chips:
        final = 2 * bit == chips
        moving = group_states(own, partner, others, bit, final, before if final else ())
        others.append(send(moving, "ctx", lambda index: index ^ (2 * bit)))
        bit *= 2
    mine, half = finished(own, partner, others, last)
    return (mine, send(half, "ctx", lambda index: index ^ 1)), others


def read_states(refs, head):
    first = lax.axis_index("ctx") % 2 == 0
    mine, theirs = refs
    return (
        jnp.concatenate(
            [
                jnp.where(first, mine[state, head], theirs[state, head]),
                jnp.where(first, theirs[state, head], mine[state, head]),
            ],
            0,
        )
        for state in range(2)
    )


def grads_kernel(parts, factor, groups, *refs):
    outputs, token, (ordered, staged, sem) = refs[-7:-4], refs[-4], refs[-3:]
    me = lax.axis_index("head")
    rows = refs[0].shape[1]
    length = parts * rows
    tiles = length // TILE
    row = lax.broadcasted_iota(jnp.int32, (TILE, TILE), 0)
    column = lax.broadcasted_iota(jnp.int32, (TILE, TILE), 1)
    low, high = column <= row, row <= column

    def scores(a, b, keep):
        value = dot(a, b, (1, 1))
        if keep is not None:
            value = jnp.where(keep, value, 0.0)
        return value.astype(BF16)

    def total(lefts, rights):
        value = dot(jnp.concatenate(lefts, 1), jnp.concatenate(rights, 0), (1, 0))
        return (value * factor).astype(BF16)

    copies = []

    def store(slot, column, index, tile, value):
        at = pl.ds(tile * TILE, TILE)
        staged[slot, index, at] = value
        copies.append(
            pltpu.make_async_copy(
                staged.at[slot, index, at],
                outputs[index].at[0, at, pl.ds(column * HD, HD)],
                sem.at[slot, index, tile],
            )
        )
        copies[-1].start()

    slot = 0
    for group, (offset, first, heads) in enumerate(groups):
        arrays = refs[group * (parts + 2) :][: parts + 2]
        received, states = arrays[:parts], arrays[parts:]
        for head in range(heads):
            for step, ref in zip(steps_of(parts), received):
                place = source_of(me, step, parts)
                for tensor in range(4):
                    ordered[slot, tensor, place] = ref[4 * head + tensor]
            key_state, query_state = read_states(states, head + offset)
            query_turned = query_state.astype(F32).T.astype(BF16)
            query, keys, values, grads = (
                ordered[slot, tensor].reshape(tiles, TILE, HD) for tensor in range(4)
            )
            for i in range(tiles):
                before, after = range(i + 1), range(i, tiles)
                column = first + head
                store(slot, column, 0, i, total(
                    [scores(grads[i], values[j], low if i == j else None) for j in before] + [grads[i]],
                    [keys[j] for j in before] + [key_state],
                ))
                store(slot, column, 1, i, total(
                    [scores(values[i], grads[j], high if i == j else None) for j in after] + [values[i]],
                    [query[j] for j in after] + [query_turned],
                ))
                store(slot, column, 2, i, total(
                    [scores(keys[i], query[j], high if i == j else None) for j in after] + [keys[i]],
                    [grads[j] for j in after] + [query_state],
                ))
            slot += 1
    for copy in copies:
        copy.wait()
    token[...] = jnp.zeros_like(token)


@jax.named_scope("gradients")
def gradients(groups, held, group, factor):
    parts = len(groups[0][0])
    rows = groups[0][0][0].shape[1]
    length = parts * rows
    heads = sum(item[-1] for item in groups)
    arrays = [value for received, states, *_ in groups for value in (*received, *states)]
    return pl.pallas_call(
        functools.partial(grads_kernel, parts, factor, [item[2:] for item in groups]),
        in_specs=[pl.BlockSpec(memory_space=pltpu.VMEM)] * len(arrays)
        + [pl.BlockSpec(memory_space=pltpu.HBM)] * len(held),
        out_specs=[pl.BlockSpec(memory_space=pltpu.HBM)] * 3 + [pl.BlockSpec(memory_space=pltpu.VMEM)],
        out_shape=[jax.ShapeDtypeStruct((1, length, group), BF16)] * 3
        + [jax.ShapeDtypeStruct((8, HD), F32)],
        scratch_shapes=[
            pltpu.VMEM((heads, 4, parts, rows, HD), BF16),
            pltpu.VMEM((heads, 3, length, HD), BF16),
            pltpu.SemaphoreType.DMA((heads, 3, length // TILE)),
        ],
        input_output_aliases={len(arrays) + index: index for index in range(len(held))},
        compiler_params=PARAMS,
        cost_estimate=cost(1000, 1024),
    )(*arrays, *held)


def shards(query, keys, values, grad_out):
    parts = lax.axis_size("head")
    spans = lax.axis_size("ctx")
    _, rows, full = query.shape
    group = full // parts
    heads = group // HD
    factor = (HD * rows * parts * spans) ** -0.5
    late = max(1, heads // 4)
    middle = (heads - late) // 2
    chunks = [heads - late - middle, middle, late]
    arrays = (query, keys, values, grad_out)
    first = pack_first(arrays, parts, heads, chunks[0], late)
    own, packed = pack_rest(arrays, parts, heads, chunks)

    def exchange(own, values):
        return [own] + [
            send(values[step - 1], "head", lambda index: target_of(index, step, parts))
            for step in steps_of(parts)[1:]
        ]

    received = [exchange(own, first)] + [exchange(values[0], values[1:]) for values in packed]
    early, arrived = exchanged(*own_states(received[0], chunks[0], late, []))
    *held, token = gradients([(received[0], early, 0, 0, chunks[0])], (), group, factor)
    *held, ready = gradients([(received[2], early, chunks[0], heads - late, late)], held, group, factor)
    second, _ = exchanged(*own_states(received[1], middle, 0, [arrived[0]]), [token], [ready])
    *held, _ = gradients([(received[1], second, 0, chunks[0], middle)], held, group, factor)
    return tuple(held)


def solution(mesh):
    spec = P("ctx", "head", None)
    out = P("ctx", None, "head")
    return jax.shard_map(
        shards, mesh=mesh, in_specs=(spec,) * 4, out_specs=(out,) * 3, check_vma=False
    )
```

```python
import functools

import jax
import jax.numpy as jnp
from jax import lax
from jax.experimental import pallas as pl
from jax.experimental.pallas import tpu as pltpu
from jax.sharding import PartitionSpec as P

HD = 128
TILE = 256
F32 = jnp.float32
BF16 = jnp.bfloat16
PARAMS = pltpu.CompilerParams(vmem_limit_bytes=40 * 1024 * 1024)


def dot(a, b, contract):
    return lax.dot_general(a, b, ((contract[:1], contract[1:]), ((), ())), preferred_element_type=F32)


def in_hbm(arrays):
    return [pltpu.with_memory_space_constraint(value, pltpu.HBM) for value in arrays]


def cost(flops, count):
    return pl.CostEstimate(flops=flops, bytes_accessed=2 * count, transcendentals=0)


def target_of(me, step, parts):
    if parts & (parts - 1) == 0:
        return me ^ step
    return (me + step) % parts


def source_of(me, step, parts):
    if parts & (parts - 1) == 0:
        return me ^ step
    return (me + parts - step) % parts


def steps_of(parts):
    return [0] + list(range(2, parts)) + [1]


def send(value, axis, target):
    count = lax.axis_size(axis)
    return lax.ppermute(value, axis, [(index, target(index)) for index in range(count)])


def copy_heads(inputs, parts, heads, step, head, count, target, at, sem):
    column = (target_of(lax.axis_index("head"), step, parts) * heads + head) * HD
    return [
        pltpu.make_async_copy(
            inputs[tensor].at[0, :, pl.ds(pl.multiple_of(column + index * HD, HD), HD)],
            target.at[at + 4 * index + tensor],
            sem,
        )
        for index in range(count)
        for tensor in range(4)
    ]


def first_kernel(parts, heads, count, late, *refs):
    inputs, outputs, (loaded, load_sem, copy_sem) = refs[:4], refs[4 : 3 + parts], refs[-3:]
    steps = range(1, parts)
    loads = [
        copy_heads(inputs, parts, heads, step, heads - late, late, loaded.at[step - 1], 0, load_sem.at[step - 1])
        for step in steps
    ]
    copies = [
        copy_heads(inputs, parts, heads, step, 0, count, outputs[step - 1], 0, copy_sem.at[step - 1])
        for step in steps
    ]
    for copy in sum(loads, []) + sum(copies, []):
        copy.start()
    for step in steps:
        for copy in loads[step - 1]:
            copy.wait()
        for index in range(late):
            query, keys, values, grads = (loaded[step - 1, 4 * index + tensor] for tensor in range(4))
            at = 4 * count + 2 * index
            outputs[step - 1][at] = dot(values, keys, (0, 0)).astype(BF16)
            outputs[step - 1][at + 1] = dot(query, grads, (0, 0)).astype(BF16)
    for copy in sum(copies, []):
        copy.wait()


@jax.named_scope("pack")
def pack_first(arrays, parts, heads, count, late):
    _, rows, full = arrays[0].shape
    units = 4 * count + 2 * late
    return pl.pallas_call(
        functools.partial(first_kernel, parts, heads, count, late),
        in_specs=[pl.BlockSpec(memory_space=pltpu.HBM)] * 4,
        out_specs=[pl.BlockSpec(memory_space=pltpu.VMEM)] * (parts - 1),
        out_shape=[jax.ShapeDtypeStruct((units, rows, HD), BF16)] * (parts - 1),
        scratch_shapes=[
            pltpu.VMEM((parts - 1, 4 * late, rows, HD), BF16),
            pltpu.SemaphoreType.DMA((parts - 1,)),
            pltpu.SemaphoreType.DMA((parts - 1,)),
        ],
        compiler_params=PARAMS,
        cost_estimate=cost(1000, 1024),
    )(*in_hbm(arrays))


def rest_kernel(parts, heads, chunks, *refs):
    inputs, outputs, (loaded, load_sem, copy_sem) = refs[:4], refs[4:-3], refs[-3:]
    late = chunks[-1]
    loads = copy_heads(inputs, parts, heads, 0, heads - late, late, loaded, 0, load_sem)
    copies, head = [], 0
    for chunk, count in enumerate(chunks):
        for step in range(parts):
            if chunk or not step:
                target = outputs[0] if not chunk else outputs[1 + (chunk - 1) * parts + step]
                copies += copy_heads(inputs, parts, heads, step, head, count, target, 0, copy_sem)
        head += count
    for copy in loads + copies:
        copy.start()
    for copy in loads:
        copy.wait()
    for index in range(late):
        query, keys, values, grads = (loaded[4 * index + tensor] for tensor in range(4))
        at = 4 * chunks[0] + 2 * index
        outputs[0][at] = dot(values, keys, (0, 0)).astype(BF16)
        outputs[0][at + 1] = dot(query, grads, (0, 0)).astype(BF16)
    for copy in copies:
        copy.wait()


@jax.named_scope("pack")
def pack_rest(arrays, parts, heads, chunks):
    _, rows, full = arrays[0].shape
    units = [4 * chunks[0] + 2 * chunks[-1]] + [4 * count for count in chunks[1:] for _ in range(parts)]
    flat = pl.pallas_call(
        functools.partial(rest_kernel, parts, heads, chunks),
        in_specs=[pl.BlockSpec(memory_space=pltpu.HBM)] * 4,
        out_specs=[pl.BlockSpec(memory_space=pltpu.VMEM)] * len(units),
        out_shape=[jax.ShapeDtypeStruct((unit, rows, HD), BF16) for unit in units],
        scratch_shapes=[
            pltpu.VMEM((4 * chunks[-1], rows, HD), BF16),
            pltpu.SemaphoreType.DMA,
            pltpu.SemaphoreType.DMA,
        ],
        compiler_params=PARAMS,
        cost_estimate=cost(1000, 1024),
    )(*in_hbm(arrays))
    return flat[0], [flat[1 + chunk * parts : 1 + (chunk + 1) * parts] for chunk in range(len(chunks) - 1)]


def state_kernel(parts, heads, extra, *refs):
    inputs, (out, give) = refs[:parts], refs[-2:]
    first = lax.axis_index("ctx") % 2 == 0
    half = HD // 2

    def share(head):
        for state in range(2):
            value = out[state, head]
            give[state, head] = jnp.where(first, value[half:], value[:half]).astype(BF16)

    for head in range(heads):
        query, keys, values, grads = (
            jnp.concatenate([ref[4 * head + tensor] for ref in inputs], 0) for tensor in range(4)
        )
        out[0, head] = dot(values, keys, (0, 0))
        out[1, head] = dot(query, grads, (0, 0))
        share(head)
    for late in range(extra):
        for state in range(2):
            at = 4 * heads + 2 * late + state
            out[state, heads + late] = sum(ref[at].astype(F32) for ref in inputs)
        share(heads + late)


@jax.named_scope("own_states")
def own_states(received, heads, extra, before):
    parts = len(received)
    rows = received[0].shape[1]
    return pl.pallas_call(
        functools.partial(state_kernel, parts, heads, extra),
        in_specs=[pl.BlockSpec(memory_space=pltpu.VMEM)] * parts
        + [pl.BlockSpec(memory_space=pl.ANY)] * len(before),
        out_shape=[
            jax.ShapeDtypeStruct((2, heads + extra, HD, HD), F32),
            jax.ShapeDtypeStruct((2, heads + extra, HD // 2, HD), BF16),
        ],
        compiler_params=PARAMS,
        cost_estimate=cost(1000, 1024),
    )(*received, *before)


def own_half(own, state):
    half = HD // 2
    first = lax.axis_index("ctx") % 2 == 0
    return jnp.where(first, own[state, :, :half], own[state, :, half:])


def group_kernel(bit, final, arrived, own, partner, *refs):
    others, out = refs[:arrived], refs[-1]
    chip = lax.axis_index("ctx") // 2
    totals = [
        own_half(own, state) + partner[state].astype(F32) + sum(ref[state].astype(F32) for ref in others)
        for state in range(2)
    ]
    if final:
        out[...] = jnp.where(chip & bit == 0, *totals).astype(BF16)
    else:
        for state in range(2):
            out[state] = totals[state].astype(BF16)


@jax.named_scope("chip_states")
def group_states(own, partner, others, bit, final, before):
    arrays = (own, partner, *others)
    shape = partner.shape[1:] if final else partner.shape
    return pl.pallas_call(
        functools.partial(group_kernel, bit, final, len(others)),
        in_specs=[pl.BlockSpec(memory_space=pltpu.VMEM)] * len(arrays)
        + [pl.BlockSpec(memory_space=pl.ANY)] * len(before),
        out_shape=jax.ShapeDtypeStruct(shape, BF16),
        compiler_params=PARAMS,
        cost_estimate=cost(1000, 1024),
    )(*arrays, *before)


def finish_kernel(arrived, own, partner, *refs):
    others, (mine, give) = refs[:arrived], refs[-2:]
    me = lax.axis_index("ctx")
    chip, core = me // 2, me % 2
    keys = query = jnp.zeros(mine.shape[1:], F32)
    for step, ref in enumerate(others):
        upper = chip & (1 << step) != 0
        pair = (ref, ref) if step == arrived - 1 else (ref.at[0], ref.at[1])
        keys = keys + jnp.where(upper, pair[0][...].astype(F32), 0.0)
        query = query + jnp.where(upper, 0.0, pair[1][...].astype(F32))
    mine[0] = (keys + jnp.where(core == 1, partner[0].astype(F32), 0.0)).astype(BF16)
    mine[1] = (query + jnp.where(core == 0, partner[1].astype(F32), 0.0)).astype(BF16)
    give[0] = (keys + jnp.where(core == 0, own_half(own, 0), 0.0)).astype(BF16)
    give[1] = (query + jnp.where(core == 1, own_half(own, 1), 0.0)).astype(BF16)


@jax.named_scope("chip_states")
def finished(own, partner, others, before):
    return pl.pallas_call(
        functools.partial(finish_kernel, len(others)),
        in_specs=[pl.BlockSpec(memory_space=pltpu.VMEM)] * (2 + len(others))
        + [pl.BlockSpec(memory_space=pl.ANY)] * len(before),
        out_shape=[jax.ShapeDtypeStruct(partner.shape, BF16)] * 2,
        compiler_params=PARAMS,
        cost_estimate=cost(1000, 1024),
    )(own, partner, *others, *before)


def exchanged(own, give, before=(), last=()):
    chips = lax.axis_size("ctx") // 2
    assert chips & (chips - 1) == 0
    partner = send(give, "ctx", lambda index: index ^ 1)
    others, bit = [], 1
    while bit < chips:
        final = 2 * bit == chips
        moving = group_states(own, partner, others, bit, final, before if final else ())
        others.append(send(moving, "ctx", lambda index: index ^ (2 * bit)))
        bit *= 2
    mine, half = finished(own, partner, others, last)
    return (mine, send(half, "ctx", lambda index: index ^ 1)), others


def read_states(refs, head):
    first = lax.axis_index("ctx") % 2 == 0
    mine, theirs = refs
    return (
        jnp.concatenate(
            [
                jnp.where(first, mine[state, head], theirs[state, head]),
                jnp.where(first, theirs[state, head], mine[state, head]),
            ],
            0,
        )
        for state in range(2)
    )


def grads_kernel(parts, factor, groups, *refs):
    outputs, token, (ordered, staged, sem) = refs[-7:-4], refs[-4], refs[-3:]
    me = lax.axis_index("head")
    rows = refs[0].shape[1]
    length = parts * rows
    tiles = length // TILE
    row = lax.broadcasted_iota(jnp.int32, (TILE, TILE), 0)
    column = lax.broadcasted_iota(jnp.int32, (TILE, TILE), 1)
    low, high = column <= row, row <= column

    def scores(a, others, diagonal, keep):
        value = dot(a, jnp.concatenate(others, 0), (1, 1))
        pieces = [value[:, j * TILE : (j + 1) * TILE] for j in range(len(others))]
        pieces[diagonal] = jnp.where(keep, pieces[diagonal], 0.0)
        return [piece.astype(BF16) for piece in pieces]

    def total(lefts, rights):
        value = dot(jnp.concatenate(lefts, 1), jnp.concatenate(rights, 0), (1, 0))
        return (value * factor).astype(BF16)

    copies = []

    def store(slot, column, index, tile, value):
        at = pl.ds(tile * TILE, TILE)
        staged[slot, index, at] = value
        copies.append(
            pltpu.make_async_copy(
                staged.at[slot, index, at],
                outputs[index].at[0, at, pl.ds(column * HD, HD)],
                sem.at[slot, index, tile],
            )
        )
        copies[-1].start()

    slot = 0
    for group, (offset, first, heads) in enumerate(groups):
        arrays = refs[group * (parts + 2) :][: parts + 2]
        received, states = arrays[:parts], arrays[parts:]
        for head in range(heads):
            for step, ref in zip(steps_of(parts), received):
                place = source_of(me, step, parts)
                for tensor in range(4):
                    ordered[slot, tensor, place] = ref[4 * head + tensor]
            key_state, query_state = read_states(states, head + offset)
            query_turned = query_state.astype(F32).T.astype(BF16)
            query, keys, values, grads = (
                ordered[slot, tensor].reshape(tiles, TILE, HD) for tensor in range(4)
            )
            for i in range(tiles):
                before, after = range(i + 1), range(i, tiles)
                column = first + head
                store(slot, column, 0, i, total(
                    scores(grads[i], [values[j] for j in before], i, low) + [grads[i]],
                    [keys[j] for j in before] + [key_state],
                ))
                store(slot, column, 1, i, total(
                    scores(values[i], [grads[j] for j in after], 0, high) + [values[i]],
                    [query[j] for j in after] + [query_turned],
                ))
                store(slot, column, 2, i, total(
                    scores(keys[i], [query[j] for j in after], 0, high) + [keys[i]],
                    [grads[j] for j in after] + [query_state],
                ))
            slot += 1
    for copy in copies:
        copy.wait()
    token[...] = jnp.zeros_like(token)


@jax.named_scope("gradients")
def gradients(groups, held, group, factor):
    parts = len(groups[0][0])
    rows = groups[0][0][0].shape[1]
    length = parts * rows
    heads = sum(item[-1] for item in groups)
    arrays = [value for received, states, *_ in groups for value in (*received, *states)]
    return pl.pallas_call(
        functools.partial(grads_kernel, parts, factor, [item[2:] for item in groups]),
        in_specs=[pl.BlockSpec(memory_space=pltpu.VMEM)] * len(arrays)
        + [pl.BlockSpec(memory_space=pltpu.HBM)] * len(held),
        out_specs=[pl.BlockSpec(memory_space=pltpu.HBM)] * 3 + [pl.BlockSpec(memory_space=pltpu.VMEM)],
        out_shape=[jax.ShapeDtypeStruct((1, length, group), BF16)] * 3
        + [jax.ShapeDtypeStruct((8, HD), F32)],
        scratch_shapes=[
            pltpu.VMEM((heads, 4, parts, rows, HD), BF16),
            pltpu.VMEM((heads, 3, length, HD), BF16),
            pltpu.SemaphoreType.DMA((heads, 3, length // TILE)),
        ],
        input_output_aliases={len(arrays) + index: index for index in range(len(held))},
        compiler_params=PARAMS,
        cost_estimate=cost(1000, 1024),
    )(*arrays, *held)


def shards(query, keys, values, grad_out):
    parts = lax.axis_size("head")
    spans = lax.axis_size("ctx")
    _, rows, full = query.shape
    group = full // parts
    heads = group // HD
    factor = (HD * rows * parts * spans) ** -0.5
    late = max(1, heads // 4)
    middle = (heads - late) // 2
    chunks = [heads - late - middle, middle, late]
    arrays = (query, keys, values, grad_out)
    first = pack_first(arrays, parts, heads, chunks[0], late)
    own, packed = pack_rest(arrays, parts, heads, chunks)

    def exchange(own, values):
        return [own] + [
            send(values[step - 1], "head", lambda index: target_of(index, step, parts))
            for step in steps_of(parts)[1:]
        ]

    received = [exchange(own, first)] + [exchange(values[0], values[1:]) for values in packed]
    early, arrived = exchanged(*own_states(received[0], chunks[0], late, []))
    *held, token = gradients([(received[0], early, 0, 0, chunks[0])], (), group, factor)
    *held, ready = gradients([(received[2], early, chunks[0], heads - late, late)], held, group, factor)
    second, _ = exchanged(*own_states(received[1], middle, 0, [arrived[0]]), [token], [ready])
    *held, _ = gradients([(received[1], second, 0, chunks[0], middle)], held, group, factor)
    return tuple(held)


def solution(mesh):
    spec = P("ctx", "head", None)
    out = P("ctx", None, "head")
    return jax.shard_map(
        shards, mesh=mesh, in_specs=(spec,) * 4, out_specs=(out,) * 3, check_vma=False
    )
```

```python
import functools

import jax
import jax.numpy as jnp
from jax import lax
from jax.experimental import pallas as pl
from jax.experimental.pallas import tpu as pltpu
from jax.sharding import PartitionSpec as P

HD = 128
TILE = 256
F32 = jnp.float32
BF16 = jnp.bfloat16
PARAMS = pltpu.CompilerParams(vmem_limit_bytes=40 * 1024 * 1024)


def dot(a, b, contract):
    return lax.dot_general(a, b, ((contract[:1], contract[1:]), ((), ())), preferred_element_type=F32)


def in_hbm(arrays):
    return [pltpu.with_memory_space_constraint(value, pltpu.HBM) for value in arrays]


def cost(flops, count):
    return pl.CostEstimate(flops=flops, bytes_accessed=2 * count, transcendentals=0)


def target_of(me, step, parts):
    if parts & (parts - 1) == 0:
        return me ^ step
    return (me + step) % parts


def source_of(me, step, parts):
    if parts & (parts - 1) == 0:
        return me ^ step
    return (me + parts - step) % parts


def steps_of(parts):
    return [0] + list(range(2, parts)) + [1]


def send(value, axis, target):
    count = lax.axis_size(axis)
    return lax.ppermute(value, axis, [(index, target(index)) for index in range(count)])


def copy_heads(inputs, parts, heads, step, head, count, target, at, sem):
    column = (target_of(lax.axis_index("head"), step, parts) * heads + head) * HD
    return [
        pltpu.make_async_copy(
            inputs[tensor].at[0, :, pl.ds(pl.multiple_of(column + index * HD, HD), HD)],
            target.at[at + 4 * index + tensor],
            sem,
        )
        for index in range(count)
        for tensor in range(4)
    ]


def first_kernel(parts, heads, count, late, *refs):
    inputs, outputs, (loaded, load_sem, copy_sem) = refs[:4], refs[4 : 3 + parts], refs[-3:]
    steps = range(1, parts)
    loads = [
        copy_heads(inputs, parts, heads, step, heads - late, late, loaded.at[step - 1], 0, load_sem.at[step - 1])
        for step in steps
    ]
    copies = [
        copy_heads(inputs, parts, heads, step, 0, count, outputs[step - 1], 0, copy_sem.at[step - 1])
        for step in steps
    ]
    for copy in sum(loads, []) + sum(copies, []):
        copy.start()
    for step in steps:
        for copy in loads[step - 1]:
            copy.wait()
        for index in range(late):
            query, keys, values, grads = (loaded[step - 1, 4 * index + tensor] for tensor in range(4))
            at = 4 * count + 2 * index
            outputs[step - 1][at] = dot(values, keys, (0, 0)).astype(BF16)
            outputs[step - 1][at + 1] = dot(query, grads, (0, 0)).astype(BF16)
    for copy in sum(copies, []):
        copy.wait()


@jax.named_scope("pack")
def pack_first(arrays, parts, heads, count, late):
    _, rows, full = arrays[0].shape
    units = 4 * count + 2 * late
    return pl.pallas_call(
        functools.partial(first_kernel, parts, heads, count, late),
        in_specs=[pl.BlockSpec(memory_space=pltpu.HBM)] * 4,
        out_specs=[pl.BlockSpec(memory_space=pltpu.VMEM)] * (parts - 1),
        out_shape=[jax.ShapeDtypeStruct((units, rows, HD), BF16)] * (parts - 1),
        scratch_shapes=[
            pltpu.VMEM((parts - 1, 4 * late, rows, HD), BF16),
            pltpu.SemaphoreType.DMA((parts - 1,)),
            pltpu.SemaphoreType.DMA((parts - 1,)),
        ],
        compiler_params=PARAMS,
        cost_estimate=cost(1000, 1024),
    )(*in_hbm(arrays))


def rest_kernel(parts, heads, chunks, *refs):
    inputs, outputs, (loaded, load_sem, copy_sem) = refs[:4], refs[4:-3], refs[-3:]
    late = chunks[-1]
    loads = copy_heads(inputs, parts, heads, 0, heads - late, late, loaded, 0, load_sem)
    copies, head = [], 0
    for chunk, count in enumerate(chunks):
        for step in range(parts):
            if chunk or not step:
                target = outputs[0] if not chunk else outputs[1 + (chunk - 1) * parts + step]
                copies += copy_heads(inputs, parts, heads, step, head, count, target, 0, copy_sem)
        head += count
    for copy in loads + copies:
        copy.start()
    for copy in loads:
        copy.wait()
    for index in range(late):
        query, keys, values, grads = (loaded[4 * index + tensor] for tensor in range(4))
        at = 4 * chunks[0] + 2 * index
        outputs[0][at] = dot(values, keys, (0, 0)).astype(BF16)
        outputs[0][at + 1] = dot(query, grads, (0, 0)).astype(BF16)
    for copy in copies:
        copy.wait()


@jax.named_scope("pack")
def pack_rest(arrays, parts, heads, chunks):
    _, rows, full = arrays[0].shape
    units = [4 * chunks[0] + 2 * chunks[-1]] + [4 * count for count in chunks[1:] for _ in range(parts)]
    flat = pl.pallas_call(
        functools.partial(rest_kernel, parts, heads, chunks),
        in_specs=[pl.BlockSpec(memory_space=pltpu.HBM)] * 4,
        out_specs=[pl.BlockSpec(memory_space=pltpu.VMEM)] * len(units),
        out_shape=[jax.ShapeDtypeStruct((unit, rows, HD), BF16) for unit in units],
        scratch_shapes=[
            pltpu.VMEM((4 * chunks[-1], rows, HD), BF16),
            pltpu.SemaphoreType.DMA,
            pltpu.SemaphoreType.DMA,
        ],
        compiler_params=PARAMS,
        cost_estimate=cost(1000, 1024),
    )(*in_hbm(arrays))
    return flat[0], [flat[1 + chunk * parts : 1 + (chunk + 1) * parts] for chunk in range(len(chunks) - 1)]


def state_kernel(parts, heads, extra, *refs):
    inputs, (out, give) = refs[:parts], refs[-2:]
    first = lax.axis_index("ctx") % 2 == 0
    half = HD // 2

    def share(head):
        for state in range(2):
            value = out[state, head]
            give[state, head] = jnp.where(first, value[half:], value[:half]).astype(BF16)

    for head in range(heads):
        query, keys, values, grads = (
            jnp.concatenate([ref[4 * head + tensor] for ref in inputs], 0) for tensor in range(4)
        )
        out[0, head] = dot(values, keys, (0, 0))
        out[1, head] = dot(query, grads, (0, 0))
        share(head)
    for late in range(extra):
        for state in range(2):
            at = 4 * heads + 2 * late + state
            out[state, heads + late] = sum(ref[at].astype(F32) for ref in inputs)
        share(heads + late)


@jax.named_scope("own_states")
def own_states(received, heads, extra, before):
    parts = len(received)
    rows = received[0].shape[1]
    return pl.pallas_call(
        functools.partial(state_kernel, parts, heads, extra),
        in_specs=[pl.BlockSpec(memory_space=pltpu.VMEM)] * parts
        + [pl.BlockSpec(memory_space=pl.ANY)] * len(before),
        out_shape=[
            jax.ShapeDtypeStruct((2, heads + extra, HD, HD), F32),
            jax.ShapeDtypeStruct((2, heads + extra, HD // 2, HD), BF16),
        ],
        compiler_params=PARAMS,
        cost_estimate=cost(1000, 1024),
    )(*received, *before)


def own_half(own, state):
    half = HD // 2
    first = lax.axis_index("ctx") % 2 == 0
    return jnp.where(first, own[state, :, :half], own[state, :, half:])


def group_kernel(bit, final, arrived, own, partner, *refs):
    others, out = refs[:arrived], refs[-1]
    chip = lax.axis_index("ctx") // 2
    totals = [
        own_half(own, state) + partner[state].astype(F32) + sum(ref[state].astype(F32) for ref in others)
        for state in range(2)
    ]
    if final:
        out[...] = jnp.where(chip & bit == 0, *totals).astype(BF16)
    else:
        for state in range(2):
            out[state] = totals[state].astype(BF16)


@jax.named_scope("chip_states")
def group_states(own, partner, others, bit, final, before):
    arrays = (own, partner, *others)
    shape = partner.shape[1:] if final else partner.shape
    return pl.pallas_call(
        functools.partial(group_kernel, bit, final, len(others)),
        in_specs=[pl.BlockSpec(memory_space=pltpu.VMEM)] * len(arrays)
        + [pl.BlockSpec(memory_space=pl.ANY)] * len(before),
        out_shape=jax.ShapeDtypeStruct(shape, BF16),
        compiler_params=PARAMS,
        cost_estimate=cost(1000, 1024),
    )(*arrays, *before)


def finish_kernel(arrived, own, partner, *refs):
    others, (mine, give) = refs[:arrived], refs[-2:]
    me = lax.axis_index("ctx")
    chip, core = me // 2, me % 2
    keys = query = jnp.zeros(mine.shape[1:], F32)
    for step, ref in enumerate(others):
        upper = chip & (1 << step) != 0
        pair = (ref, ref) if step == arrived - 1 else (ref.at[0], ref.at[1])
        keys = keys + jnp.where(upper, pair[0][...].astype(F32), 0.0)
        query = query + jnp.where(upper, 0.0, pair[1][...].astype(F32))
    mine[0] = (keys + jnp.where(core == 1, partner[0].astype(F32), 0.0)).astype(BF16)
    mine[1] = (query + jnp.where(core == 0, partner[1].astype(F32), 0.0)).astype(BF16)
    give[0] = (keys + jnp.where(core == 0, own_half(own, 0), 0.0)).astype(BF16)
    give[1] = (query + jnp.where(core == 1, own_half(own, 1), 0.0)).astype(BF16)


@jax.named_scope("chip_states")
def finished(own, partner, others, before):
    return pl.pallas_call(
        functools.partial(finish_kernel, len(others)),
        in_specs=[pl.BlockSpec(memory_space=pltpu.VMEM)] * (2 + len(others))
        + [pl.BlockSpec(memory_space=pl.ANY)] * len(before),
        out_shape=[jax.ShapeDtypeStruct(partner.shape, BF16)] * 2,
        compiler_params=PARAMS,
        cost_estimate=cost(1000, 1024),
    )(own, partner, *others, *before)


def exchanged(own, give, before=(), last=()):
    chips = lax.axis_size("ctx") // 2
    assert chips & (chips - 1) == 0
    partner = send(give, "ctx", lambda index: index ^ 1)
    others, bit = [], 1
    while bit < chips:
        final = 2 * bit == chips
        moving = group_states(own, partner, others, bit, final, before if final else ())
        others.append(send(moving, "ctx", lambda index: index ^ (2 * bit)))
        bit *= 2
    mine, half = finished(own, partner, others, last)
    return (mine, send(half, "ctx", lambda index: index ^ 1)), others


def read_states(refs, head):
    first = lax.axis_index("ctx") % 2 == 0
    mine, theirs = refs
    return (
        jnp.concatenate(
            [
                jnp.where(first, mine[state, head], theirs[state, head]),
                jnp.where(first, theirs[state, head], mine[state, head]),
            ],
            0,
        )
        for state in range(2)
    )


def grads_kernel(parts, factor, groups, *refs):
    outputs, token, (ordered, staged, sem) = refs[-7:-4], refs[-4], refs[-3:]
    me = lax.axis_index("head")
    rows = refs[0].shape[1]
    length = parts * rows
    tiles = length // TILE
    row = lax.broadcasted_iota(jnp.int32, (TILE, TILE), 0)
    column = lax.broadcasted_iota(jnp.int32, (TILE, TILE), 1)
    low, high = column <= row, row <= column

    def scores(a, b, keep):
        value = dot(a, b, (1, 1))
        if keep is not None:
            value = jnp.where(keep, value, 0.0)
        return value.astype(BF16)

    def total(lefts, rights):
        value = dot(jnp.concatenate(lefts, 1), jnp.concatenate(rights, 0), (1, 0))
        return (value * factor).astype(BF16)

    copies = []

    def store(slot, column, index, tile, value):
        at = pl.ds(tile * TILE, TILE)
        staged[slot, index, at] = value
        copies.append(
            pltpu.make_async_copy(
                staged.at[slot, index, at],
                outputs[index].at[0, at, pl.ds(column * HD, HD)],
                sem.at[slot, index, tile],
            )
        )
        copies[-1].start()

    slot = 0
    for group, (offset, first, heads) in enumerate(groups):
        arrays = refs[group * (parts + 2) :][: parts + 2]
        received, states = arrays[:parts], arrays[parts:]
        for head in range(heads):
            for step, ref in zip(steps_of(parts), received):
                place = source_of(me, step, parts)
                for tensor in range(4):
                    ordered[slot, tensor, place] = ref[4 * head + tensor]
            key_state, query_state = read_states(states, head + offset)
            query_turned = query_state.astype(F32).T.astype(BF16)
            query, keys, values, grads = (
                ordered[slot, tensor].reshape(tiles, TILE, HD) for tensor in range(4)
            )
            for i in range(tiles):
                before, after = range(i + 1), range(i, tiles)
                column = first + head
                store(slot, column, 0, i, total(
                    [scores(grads[i], values[j], low if i == j else None) for j in before] + [grads[i]],
                    [keys[j] for j in before] + [key_state],
                ))
                store(slot, column, 1, i, total(
                    [scores(values[i], grads[j], high if i == j else None) for j in after] + [values[i]],
                    [query[j] for j in after] + [query_turned],
                ))
                store(slot, column, 2, i, total(
                    [scores(keys[i], query[j], high if i == j else None) for j in after] + [keys[i]],
                    [grads[j] for j in after] + [query_state],
                ))
            slot += 1
    for copy in copies:
        copy.wait()
    token[...] = jnp.zeros_like(token)


@jax.named_scope("gradients")
def gradients(groups, held, group, factor):
    parts = len(groups[0][0])
    rows = groups[0][0][0].shape[1]
    length = parts * rows
    heads = sum(item[-1] for item in groups)
    arrays = [value for received, states, *_ in groups for value in (*received, *states)]
    return pl.pallas_call(
        functools.partial(grads_kernel, parts, factor, [item[2:] for item in groups]),
        in_specs=[pl.BlockSpec(memory_space=pltpu.VMEM)] * len(arrays)
        + [pl.BlockSpec(memory_space=pltpu.HBM)] * len(held),
        out_specs=[pl.BlockSpec(memory_space=pltpu.HBM)] * 3 + [pl.BlockSpec(memory_space=pltpu.VMEM)],
        out_shape=[jax.ShapeDtypeStruct((1, length, group), BF16)] * 3
        + [jax.ShapeDtypeStruct((8, HD), F32)],
        scratch_shapes=[
            pltpu.VMEM((heads, 4, parts, rows, HD), BF16),
            pltpu.VMEM((heads, 3, length, HD), BF16),
            pltpu.SemaphoreType.DMA((heads, 3, length // TILE)),
        ],
        input_output_aliases={len(arrays) + index: index for index in range(len(held))},
        compiler_params=PARAMS,
        cost_estimate=cost(1000, 1024),
    )(*arrays, *held)


def shards(query, keys, values, grad_out):
    parts = lax.axis_size("head")
    spans = lax.axis_size("ctx")
    _, rows, full = query.shape
    group = full // parts
    heads = group // HD
    factor = (HD * rows * parts * spans) ** -0.5
    late, middle = max(1, heads // 4), max(1, heads * 3 // 8)
    chunks = [heads - late - middle, middle, late]
    arrays = (query, keys, values, grad_out)
    first = pack_first(arrays, parts, heads, chunks[0], late)
    own, packed = pack_rest(arrays, parts, heads, chunks)

    def exchange(own, values):
        return [own] + [
            send(values[step - 1], "head", lambda index: target_of(index, step, parts))
            for step in steps_of(parts)[1:]
        ]

    received = [exchange(own, first)] + [exchange(values[0], values[1:]) for values in packed]
    early, arrived = exchanged(*own_states(received[0], chunks[0], late, []))
    *held, token = gradients([(received[0], early, 0, 0, chunks[0])], (), group, factor)
    *held, ready = gradients([(received[2], early, chunks[0], heads - late, late)], held, group, factor)
    second, _ = exchanged(*own_states(received[1], middle, 0, [arrived[0]]), [token, received[2][1]], [ready])
    *held, _ = gradients([(received[1], second, 0, chunks[0], middle)], held, group, factor)
    return tuple(held)


def solution(mesh):
    spec = P("ctx", "head", None)
    out = P("ctx", None, "head")
    return jax.shard_map(
        shards, mesh=mesh, in_specs=(spec,) * 4, out_specs=(out,) * 3, check_vma=False
    )
```

```python
import functools

import jax
import jax.numpy as jnp
from jax import lax
from jax.experimental import pallas as pl
from jax.experimental.pallas import tpu as pltpu
from jax.sharding import PartitionSpec as P

HD = 128
TILE = 256
F32 = jnp.float32
BF16 = jnp.bfloat16
PARAMS = pltpu.CompilerParams(vmem_limit_bytes=40 * 1024 * 1024)


def dot(a, b, contract):
    return lax.dot_general(a, b, ((contract[:1], contract[1:]), ((), ())), preferred_element_type=F32)


def in_hbm(arrays):
    return [pltpu.with_memory_space_constraint(value, pltpu.HBM) for value in arrays]


def cost(flops, count):
    return pl.CostEstimate(flops=flops, bytes_accessed=2 * count, transcendentals=0)


def target_of(me, step, parts):
    if parts & (parts - 1) == 0:
        return me ^ step
    return (me + step) % parts


def source_of(me, step, parts):
    if parts & (parts - 1) == 0:
        return me ^ step
    return (me + parts - step) % parts


def steps_of(parts):
    return [0] + list(range(2, parts)) + [1]


def send(value, axis, target):
    count = lax.axis_size(axis)
    return lax.ppermute(value, axis, [(index, target(index)) for index in range(count)])


def copy_heads(inputs, parts, heads, step, head, count, target, at, sem):
    column = (target_of(lax.axis_index("head"), step, parts) * heads + head) * HD
    return [
        pltpu.make_async_copy(
            inputs[tensor].at[0, :, pl.ds(pl.multiple_of(column + index * HD, HD), HD)],
            target.at[at + 4 * index + tensor],
            sem,
        )
        for index in range(count)
        for tensor in range(4)
    ]


def first_kernel(parts, heads, count, late, *refs):
    inputs, outputs, (loaded, load_sem, copy_sem) = refs[:4], refs[4 : 3 + parts], refs[-3:]
    steps = range(1, parts)
    loads = [
        copy_heads(inputs, parts, heads, step, heads - late, late, loaded.at[step - 1], 0, load_sem.at[step - 1])
        for step in steps
    ]
    copies = [
        copy_heads(inputs, parts, heads, step, 0, count, outputs[step - 1], 0, copy_sem.at[step - 1])
        for step in steps
    ]
    for copy in sum(loads, []) + sum(copies, []):
        copy.start()
    for step in steps:
        for copy in loads[step - 1]:
            copy.wait()
        for index in range(late):
            query, keys, values, grads = (loaded[step - 1, 4 * index + tensor] for tensor in range(4))
            at = 4 * count + 2 * index
            outputs[step - 1][at] = dot(values, keys, (0, 0)).astype(BF16)
            outputs[step - 1][at + 1] = dot(query, grads, (0, 0)).astype(BF16)
    for copy in sum(copies, []):
        copy.wait()


@jax.named_scope("pack")
def pack_first(arrays, parts, heads, count, late):
    _, rows, full = arrays[0].shape
    units = 4 * count + 2 * late
    return pl.pallas_call(
        functools.partial(first_kernel, parts, heads, count, late),
        in_specs=[pl.BlockSpec(memory_space=pltpu.HBM)] * 4,
        out_specs=[pl.BlockSpec(memory_space=pltpu.VMEM)] * (parts - 1),
        out_shape=[jax.ShapeDtypeStruct((units, rows, HD), BF16)] * (parts - 1),
        scratch_shapes=[
            pltpu.VMEM((parts - 1, 4 * late, rows, HD), BF16),
            pltpu.SemaphoreType.DMA((parts - 1,)),
            pltpu.SemaphoreType.DMA((parts - 1,)),
        ],
        compiler_params=PARAMS,
        cost_estimate=cost(1000, 1024),
    )(*in_hbm(arrays))


def rest_kernel(parts, heads, chunks, *refs):
    inputs, outputs, (loaded, load_sem, copy_sem) = refs[:4], refs[4:-3], refs[-3:]
    late = chunks[-1]
    loads = copy_heads(inputs, parts, heads, 0, heads - late, late, loaded, 0, load_sem)
    copies, head = [], 0
    for chunk, count in enumerate(chunks):
        for step in range(parts):
            if chunk or not step:
                target = outputs[0] if not chunk else outputs[1 + (chunk - 1) * parts + step]
                copies += copy_heads(inputs, parts, heads, step, head, count, target, 0, copy_sem)
        head += count
    for copy in loads + copies:
        copy.start()
    for copy in loads:
        copy.wait()
    for index in range(late):
        query, keys, values, grads = (loaded[4 * index + tensor] for tensor in range(4))
        at = 4 * chunks[0] + 2 * index
        outputs[0][at] = dot(values, keys, (0, 0)).astype(BF16)
        outputs[0][at + 1] = dot(query, grads, (0, 0)).astype(BF16)
    for copy in copies:
        copy.wait()


@jax.named_scope("pack")
def pack_rest(arrays, parts, heads, chunks):
    _, rows, full = arrays[0].shape
    units = [4 * chunks[0] + 2 * chunks[-1]] + [4 * count for count in chunks[1:] for _ in range(parts)]
    flat = pl.pallas_call(
        functools.partial(rest_kernel, parts, heads, chunks),
        in_specs=[pl.BlockSpec(memory_space=pltpu.HBM)] * 4,
        out_specs=[pl.BlockSpec(memory_space=pltpu.VMEM)] * len(units),
        out_shape=[jax.ShapeDtypeStruct((unit, rows, HD), BF16) for unit in units],
        scratch_shapes=[
            pltpu.VMEM((4 * chunks[-1], rows, HD), BF16),
            pltpu.SemaphoreType.DMA,
            pltpu.SemaphoreType.DMA,
        ],
        compiler_params=PARAMS,
        cost_estimate=cost(1000, 1024),
    )(*in_hbm(arrays))
    return flat[0], [flat[1 + chunk * parts : 1 + (chunk + 1) * parts] for chunk in range(len(chunks) - 1)]


def state_kernel(parts, heads, extra, *refs):
    inputs, (out, give) = refs[:parts], refs[-2:]
    first = lax.axis_index("ctx") % 2 == 0
    half = HD // 2

    def share(head):
        for state in range(2):
            value = out[state, head]
            give[state, head] = jnp.where(first, value[half:], value[:half]).astype(BF16)

    for head in range(heads):
        query, keys, values, grads = (
            jnp.concatenate([ref[4 * head + tensor] for ref in inputs], 0) for tensor in range(4)
        )
        out[0, head] = dot(values, keys, (0, 0))
        out[1, head] = dot(query, grads, (0, 0))
        share(head)
    for late in range(extra):
        for state in range(2):
            at = 4 * heads + 2 * late + state
            out[state, heads + late] = sum(ref[at].astype(F32) for ref in inputs)
        share(heads + late)


@jax.named_scope("own_states")
def own_states(received, heads, extra, before):
    parts = len(received)
    rows = received[0].shape[1]
    return pl.pallas_call(
        functools.partial(state_kernel, parts, heads, extra),
        in_specs=[pl.BlockSpec(memory_space=pltpu.VMEM)] * parts
        + [pl.BlockSpec(memory_space=pl.ANY)] * len(before),
        out_shape=[
            jax.ShapeDtypeStruct((2, heads + extra, HD, HD), F32),
            jax.ShapeDtypeStruct((2, heads + extra, HD // 2, HD), BF16),
        ],
        compiler_params=PARAMS,
        cost_estimate=cost(1000, 1024),
    )(*received, *before)


def own_half(own, state):
    half = HD // 2
    first = lax.axis_index("ctx") % 2 == 0
    return jnp.where(first, own[state, :, :half], own[state, :, half:])


def group_kernel(bit, final, arrived, own, partner, *refs):
    others, out = refs[:arrived], refs[-1]
    chip = lax.axis_index("ctx") // 2
    totals = [
        own_half(own, state) + partner[state].astype(F32) + sum(ref[state].astype(F32) for ref in others)
        for state in range(2)
    ]
    if final:
        out[...] = jnp.where(chip & bit == 0, *totals).astype(BF16)
    else:
        for state in range(2):
            out[state] = totals[state].astype(BF16)


@jax.named_scope("chip_states")
def group_states(own, partner, others, bit, final, before):
    arrays = (own, partner, *others)
    shape = partner.shape[1:] if final else partner.shape
    return pl.pallas_call(
        functools.partial(group_kernel, bit, final, len(others)),
        in_specs=[pl.BlockSpec(memory_space=pltpu.VMEM)] * len(arrays)
        + [pl.BlockSpec(memory_space=pl.ANY)] * len(before),
        out_shape=jax.ShapeDtypeStruct(shape, BF16),
        compiler_params=PARAMS,
        cost_estimate=cost(1000, 1024),
    )(*arrays, *before)


def finish_kernel(arrived, own, partner, *refs):
    others, (mine, give) = refs[:arrived], refs[-2:]
    me = lax.axis_index("ctx")
    chip, core = me // 2, me % 2
    keys = query = jnp.zeros(mine.shape[1:], F32)
    for step, ref in enumerate(others):
        upper = chip & (1 << step) != 0
        pair = (ref, ref) if step == arrived - 1 else (ref.at[0], ref.at[1])
        keys = keys + jnp.where(upper, pair[0][...].astype(F32), 0.0)
        query = query + jnp.where(upper, 0.0, pair[1][...].astype(F32))
    mine[0] = (keys + jnp.where(core == 1, partner[0].astype(F32), 0.0)).astype(BF16)
    mine[1] = (query + jnp.where(core == 0, partner[1].astype(F32), 0.0)).astype(BF16)
    give[0] = (keys + jnp.where(core == 0, own_half(own, 0), 0.0)).astype(BF16)
    give[1] = (query + jnp.where(core == 1, own_half(own, 1), 0.0)).astype(BF16)


@jax.named_scope("chip_states")
def finished(own, partner, others, before):
    return pl.pallas_call(
        functools.partial(finish_kernel, len(others)),
        in_specs=[pl.BlockSpec(memory_space=pltpu.VMEM)] * (2 + len(others))
        + [pl.BlockSpec(memory_space=pl.ANY)] * len(before),
        out_shape=[jax.ShapeDtypeStruct(partner.shape, BF16)] * 2,
        compiler_params=PARAMS,
        cost_estimate=cost(1000, 1024),
    )(own, partner, *others, *before)


def exchanged(own, give, before=(), last=()):
    chips = lax.axis_size("ctx") // 2
    assert chips & (chips - 1) == 0
    partner = send(give, "ctx", lambda index: index ^ 1)
    others, bit = [], 1
    while bit < chips:
        final = 2 * bit == chips
        moving = group_states(own, partner, others, bit, final, before if final else ())
        others.append(send(moving, "ctx", lambda index: index ^ (2 * bit)))
        bit *= 2
    mine, half = finished(own, partner, others, last)
    return (mine, send(half, "ctx", lambda index: index ^ 1)), others


def read_states(refs, head):
    first = lax.axis_index("ctx") % 2 == 0
    mine, theirs = refs
    return (
        jnp.concatenate(
            [
                jnp.where(first, mine[state, head], theirs[state, head]),
                jnp.where(first, theirs[state, head], mine[state, head]),
            ],
            0,
        )
        for state in range(2)
    )


def grads_kernel(parts, factor, groups, *refs):
    outputs, token, (ordered, staged, sem) = refs[-7:-4], refs[-4], refs[-3:]
    me = lax.axis_index("head")
    rows = refs[0].shape[1]
    length = parts * rows
    tiles = length // TILE
    row = lax.broadcasted_iota(jnp.int32, (TILE, TILE), 0)
    column = lax.broadcasted_iota(jnp.int32, (TILE, TILE), 1)
    low, high = column <= row, row <= column

    def scores(a, b, keep):
        value = dot(a, b, (1, 1))
        if keep is not None:
            value = jnp.where(keep, value, 0.0)
        return value.astype(BF16)

    def total(lefts, rights):
        value = dot(jnp.concatenate(lefts, 1), jnp.concatenate(rights, 0), (1, 0))
        return (value * factor).astype(BF16)

    copies = []

    def store(slot, column, index, tile, value):
        at = pl.ds(tile * TILE, TILE)
        staged[slot, index, at] = value
        copies.append(
            pltpu.make_async_copy(
                staged.at[slot, index, at],
                outputs[index].at[0, at, pl.ds(column * HD, HD)],
                sem.at[slot, index, tile],
            )
        )
        copies[-1].start()

    slot = 0
    for group, (offset, first, heads) in enumerate(groups):
        arrays = refs[group * (parts + 2) :][: parts + 2]
        received, states = arrays[:parts], arrays[parts:]
        for head in range(heads):
            for step, ref in zip(steps_of(parts), received):
                place = source_of(me, step, parts)
                for tensor in range(4):
                    ordered[slot, tensor, place] = ref[4 * head + tensor]
            key_state, query_state = read_states(states, head + offset)
            query_turned = query_state.astype(F32).T.astype(BF16)
            query, keys, values, grads = (
                ordered[slot, tensor].reshape(tiles, TILE, HD) for tensor in range(4)
            )
            for i in range(tiles):
                before, after = range(i + 1), range(i, tiles)
                column = first + head
                store(slot, column, 0, i, total(
                    [scores(grads[i], values[j], low if i == j else None) for j in before] + [grads[i]],
                    [keys[j] for j in before] + [key_state],
                ))
                store(slot, column, 1, i, total(
                    [scores(values[i], grads[j], high if i == j else None) for j in after] + [values[i]],
                    [query[j] for j in after] + [query_turned],
                ))
                store(slot, column, 2, i, total(
                    [scores(keys[i], query[j], high if i == j else None) for j in after] + [keys[i]],
                    [grads[j] for j in after] + [query_state],
                ))
            slot += 1
    for copy in copies:
        copy.wait()
    token[...] = jnp.zeros_like(token)


@jax.named_scope("gradients")
def gradients(groups, held, group, factor):
    parts = len(groups[0][0])
    rows = groups[0][0][0].shape[1]
    length = parts * rows
    heads = sum(item[-1] for item in groups)
    arrays = [value for received, states, *_ in groups for value in (*received, *states)]
    return pl.pallas_call(
        functools.partial(grads_kernel, parts, factor, [item[2:] for item in groups]),
        in_specs=[pl.BlockSpec(memory_space=pltpu.VMEM)] * len(arrays)
        + [pl.BlockSpec(memory_space=pltpu.HBM)] * len(held),
        out_specs=[pl.BlockSpec(memory_space=pltpu.HBM)] * 3 + [pl.BlockSpec(memory_space=pltpu.VMEM)],
        out_shape=[jax.ShapeDtypeStruct((1, length, group), BF16)] * 3
        + [jax.ShapeDtypeStruct((8, HD), F32)],
        scratch_shapes=[
            pltpu.VMEM((heads, 4, parts, rows, HD), BF16),
            pltpu.VMEM((heads, 3, length, HD), BF16),
            pltpu.SemaphoreType.DMA((heads, 3, length // TILE)),
        ],
        input_output_aliases={len(arrays) + index: index for index in range(len(held))},
        compiler_params=PARAMS,
        cost_estimate=cost(1000, 1024),
    )(*arrays, *held)


def shards(query, keys, values, grad_out):
    parts = lax.axis_size("head")
    spans = lax.axis_size("ctx")
    _, rows, full = query.shape
    group = full // parts
    heads = group // HD
    factor = (HD * rows * parts * spans) ** -0.5
    late, middle = max(1, heads // 4), max(1, heads * 3 // 8)
    chunks = [heads - late - middle, middle, late]
    arrays = (query, keys, values, grad_out)
    first = pack_first(arrays, parts, heads, chunks[0], late)
    own, packed = pack_rest(arrays, parts, heads, chunks)

    def exchange(own, values):
        return [own] + [
            send(values[step - 1], "head", lambda index: target_of(index, step, parts))
            for step in steps_of(parts)[1:]
        ]

    received = [exchange(own, first)] + [exchange(values[0], values[1:]) for values in packed]
    early, arrived = exchanged(*own_states(received[0], chunks[0], late, []))
    *held, token = gradients([(received[0], early, 0, 0, chunks[0])], (), group, factor)
    second, _ = exchanged(*own_states(received[1], middle, 0, [arrived[0]]), [token], received[2][1:2])
    *held, _ = gradients(
        [
            (received[1], second, 0, chunks[0], middle),
            (received[2], early, chunks[0], heads - late, late),
        ],
        held,
        group,
        factor,
    )
    return tuple(held)


def solution(mesh):
    spec = P("ctx", "head", None)
    out = P("ctx", None, "head")
    return jax.shard_map(
        shards, mesh=mesh, in_specs=(spec,) * 4, out_specs=(out,) * 3, check_vma=False
    )
```

```python
import functools

import jax
import jax.numpy as jnp
from jax import lax
from jax.experimental import pallas as pl
from jax.experimental.pallas import tpu as pltpu
from jax.sharding import PartitionSpec as P

HD = 128
TILE = 512
F32 = jnp.float32
BF16 = jnp.bfloat16
PARAMS = pltpu.CompilerParams(vmem_limit_bytes=40 * 1024 * 1024)


def dot(a, b, contract):
    return lax.dot_general(a, b, ((contract[:1], contract[1:]), ((), ())), preferred_element_type=F32)


def in_hbm(arrays):
    return [pltpu.with_memory_space_constraint(value, pltpu.HBM) for value in arrays]


def cost(flops, count):
    return pl.CostEstimate(flops=flops, bytes_accessed=2 * count, transcendentals=0)


def target_of(me, step, parts):
    if parts & (parts - 1) == 0:
        return me ^ step
    return (me + step) % parts


def source_of(me, step, parts):
    if parts & (parts - 1) == 0:
        return me ^ step
    return (me + parts - step) % parts


def steps_of(parts):
    return [0] + list(range(2, parts)) + [1]


def send(value, axis, target):
    count = lax.axis_size(axis)
    return lax.ppermute(value, axis, [(index, target(index)) for index in range(count)])


def copy_heads(inputs, parts, heads, step, head, count, target, at, sem):
    column = (target_of(lax.axis_index("head"), step, parts) * heads + head) * HD
    return [
        pltpu.make_async_copy(
            inputs[tensor].at[0, :, pl.ds(pl.multiple_of(column + index * HD, HD), HD)],
            target.at[at + 4 * index + tensor],
            sem,
        )
        for index in range(count)
        for tensor in range(4)
    ]


def first_kernel(parts, heads, count, late, *refs):
    inputs, outputs, (loaded, load_sem, copy_sem) = refs[:4], refs[4 : 3 + parts], refs[-3:]
    steps = range(1, parts)
    loads = [
        copy_heads(inputs, parts, heads, step, heads - late, late, loaded.at[step - 1], 0, load_sem.at[step - 1])
        for step in steps
    ]
    copies = [
        copy_heads(inputs, parts, heads, step, 0, count, outputs[step - 1], 0, copy_sem.at[step - 1])
        for step in steps
    ]
    for copy in sum(loads, []) + sum(copies, []):
        copy.start()
    for step in steps:
        for copy in loads[step - 1]:
            copy.wait()
        for index in range(late):
            query, keys, values, grads = (loaded[step - 1, 4 * index + tensor] for tensor in range(4))
            at = 4 * count + 2 * index
            outputs[step - 1][at] = dot(values, keys, (0, 0)).astype(BF16)
            outputs[step - 1][at + 1] = dot(query, grads, (0, 0)).astype(BF16)
    for copy in sum(copies, []):
        copy.wait()


@jax.named_scope("pack")
def pack_first(arrays, parts, heads, count, late):
    _, rows, full = arrays[0].shape
    units = 4 * count + 2 * late
    return pl.pallas_call(
        functools.partial(first_kernel, parts, heads, count, late),
        in_specs=[pl.BlockSpec(memory_space=pltpu.HBM)] * 4,
        out_specs=[pl.BlockSpec(memory_space=pltpu.VMEM)] * (parts - 1),
        out_shape=[jax.ShapeDtypeStruct((units, rows, HD), BF16)] * (parts - 1),
        scratch_shapes=[
            pltpu.VMEM((parts - 1, 4 * late, rows, HD), BF16),
            pltpu.SemaphoreType.DMA((parts - 1,)),
            pltpu.SemaphoreType.DMA((parts - 1,)),
        ],
        compiler_params=PARAMS,
        cost_estimate=cost(1000, 1024),
    )(*in_hbm(arrays))


def rest_kernel(parts, heads, chunks, *refs):
    inputs, outputs, (loaded, load_sem, copy_sem) = refs[:4], refs[4:-3], refs[-3:]
    late = chunks[-1]
    loads = copy_heads(inputs, parts, heads, 0, heads - late, late, loaded, 0, load_sem)
    copies, head = [], 0
    for chunk, count in enumerate(chunks):
        for step in range(parts):
            if chunk or not step:
                target = outputs[0] if not chunk else outputs[1 + (chunk - 1) * parts + step]
                copies += copy_heads(inputs, parts, heads, step, head, count, target, 0, copy_sem)
        head += count
    for copy in loads + copies:
        copy.start()
    for copy in loads:
        copy.wait()
    for index in range(late):
        query, keys, values, grads = (loaded[4 * index + tensor] for tensor in range(4))
        at = 4 * chunks[0] + 2 * index
        outputs[0][at] = dot(values, keys, (0, 0)).astype(BF16)
        outputs[0][at + 1] = dot(query, grads, (0, 0)).astype(BF16)
    for copy in copies:
        copy.wait()


@jax.named_scope("pack")
def pack_rest(arrays, parts, heads, chunks):
    _, rows, full = arrays[0].shape
    units = [4 * chunks[0] + 2 * chunks[-1]] + [4 * count for count in chunks[1:] for _ in range(parts)]
    flat = pl.pallas_call(
        functools.partial(rest_kernel, parts, heads, chunks),
        in_specs=[pl.BlockSpec(memory_space=pltpu.HBM)] * 4,
        out_specs=[pl.BlockSpec(memory_space=pltpu.VMEM)] * len(units),
        out_shape=[jax.ShapeDtypeStruct((unit, rows, HD), BF16) for unit in units],
        scratch_shapes=[
            pltpu.VMEM((4 * chunks[-1], rows, HD), BF16),
            pltpu.SemaphoreType.DMA,
            pltpu.SemaphoreType.DMA,
        ],
        compiler_params=PARAMS,
        cost_estimate=cost(1000, 1024),
    )(*in_hbm(arrays))
    return flat[0], [flat[1 + chunk * parts : 1 + (chunk + 1) * parts] for chunk in range(len(chunks) - 1)]


def state_kernel(parts, heads, extra, *refs):
    inputs, (out, give) = refs[:parts], refs[-2:]
    first = lax.axis_index("ctx") % 2 == 0
    half = HD // 2

    def share(head):
        for state in range(2):
            value = out[state, head]
            give[state, head] = jnp.where(first, value[half:], value[:half]).astype(BF16)

    for head in range(heads):
        query, keys, values, grads = (
            jnp.concatenate([ref[4 * head + tensor] for ref in inputs], 0) for tensor in range(4)
        )
        out[0, head] = dot(values, keys, (0, 0))
        out[1, head] = dot(query, grads, (0, 0))
        share(head)
    for late in range(extra):
        for state in range(2):
            at = 4 * heads + 2 * late + state
            out[state, heads + late] = sum(ref[at].astype(F32) for ref in inputs)
        share(heads + late)


@jax.named_scope("own_states")
def own_states(received, heads, extra, before):
    parts = len(received)
    rows = received[0].shape[1]
    return pl.pallas_call(
        functools.partial(state_kernel, parts, heads, extra),
        in_specs=[pl.BlockSpec(memory_space=pltpu.VMEM)] * parts
        + [pl.BlockSpec(memory_space=pl.ANY)] * len(before),
        out_shape=[
            jax.ShapeDtypeStruct((2, heads + extra, HD, HD), F32),
            jax.ShapeDtypeStruct((2, heads + extra, HD // 2, HD), BF16),
        ],
        compiler_params=PARAMS,
        cost_estimate=cost(1000, 1024),
    )(*received, *before)


def own_half(own, state):
    half = HD // 2
    first = lax.axis_index("ctx") % 2 == 0
    return jnp.where(first, own[state, :, :half], own[state, :, half:])


def group_kernel(bit, final, arrived, own, partner, *refs):
    others, out = refs[:arrived], refs[-1]
    chip = lax.axis_index("ctx") // 2
    totals = [
        own_half(own, state) + partner[state].astype(F32) + sum(ref[state].astype(F32) for ref in others)
        for state in range(2)
    ]
    if final:
        out[...] = jnp.where(chip & bit == 0, *totals).astype(BF16)
    else:
        for state in range(2):
            out[state] = totals[state].astype(BF16)


@jax.named_scope("chip_states")
def group_states(own, partner, others, bit, final, before):
    arrays = (own, partner, *others)
    shape = partner.shape[1:] if final else partner.shape
    return pl.pallas_call(
        functools.partial(group_kernel, bit, final, len(others)),
        in_specs=[pl.BlockSpec(memory_space=pltpu.VMEM)] * len(arrays)
        + [pl.BlockSpec(memory_space=pl.ANY)] * len(before),
        out_shape=jax.ShapeDtypeStruct(shape, BF16),
        compiler_params=PARAMS,
        cost_estimate=cost(1000, 1024),
    )(*arrays, *before)


def finish_kernel(arrived, own, partner, *refs):
    others, (mine, give) = refs[:arrived], refs[-2:]
    me = lax.axis_index("ctx")
    chip, core = me // 2, me % 2
    keys = query = jnp.zeros(mine.shape[1:], F32)
    for step, ref in enumerate(others):
        upper = chip & (1 << step) != 0
        pair = (ref, ref) if step == arrived - 1 else (ref.at[0], ref.at[1])
        keys = keys + jnp.where(upper, pair[0][...].astype(F32), 0.0)
        query = query + jnp.where(upper, 0.0, pair[1][...].astype(F32))
    mine[0] = (keys + jnp.where(core == 1, partner[0].astype(F32), 0.0)).astype(BF16)
    mine[1] = (query + jnp.where(core == 0, partner[1].astype(F32), 0.0)).astype(BF16)
    give[0] = (keys + jnp.where(core == 0, own_half(own, 0), 0.0)).astype(BF16)
    give[1] = (query + jnp.where(core == 1, own_half(own, 1), 0.0)).astype(BF16)


@jax.named_scope("chip_states")
def finished(own, partner, others, before):
    return pl.pallas_call(
        functools.partial(finish_kernel, len(others)),
        in_specs=[pl.BlockSpec(memory_space=pltpu.VMEM)] * (2 + len(others))
        + [pl.BlockSpec(memory_space=pl.ANY)] * len(before),
        out_shape=[jax.ShapeDtypeStruct(partner.shape, BF16)] * 2,
        compiler_params=PARAMS,
        cost_estimate=cost(1000, 1024),
    )(own, partner, *others, *before)


def exchanged(own, give, before=(), last=()):
    chips = lax.axis_size("ctx") // 2
    assert chips & (chips - 1) == 0
    partner = send(give, "ctx", lambda index: index ^ 1)
    others, bit = [], 1
    while bit < chips:
        final = 2 * bit == chips
        moving = group_states(own, partner, others, bit, final, before if final else ())
        others.append(send(moving, "ctx", lambda index: index ^ (2 * bit)))
        bit *= 2
    mine, half = finished(own, partner, others, last)
    return (mine, send(half, "ctx", lambda index: index ^ 1)), others


def read_states(refs, head):
    first = lax.axis_index("ctx") % 2 == 0
    mine, theirs = refs
    return (
        jnp.concatenate(
            [
                jnp.where(first, mine[state, head], theirs[state, head]),
                jnp.where(first, theirs[state, head], mine[state, head]),
            ],
            0,
        )
        for state in range(2)
    )


def grads_kernel(parts, factor, groups, *refs):
    outputs, token, (ordered, staged, sem) = refs[-7:-4], refs[-4], refs[-3:]
    me = lax.axis_index("head")
    rows = refs[0].shape[1]
    length = parts * rows
    tiles = length // TILE
    row = lax.broadcasted_iota(jnp.int32, (TILE, TILE), 0)
    column = lax.broadcasted_iota(jnp.int32, (TILE, TILE), 1)
    low, high = column <= row, row <= column

    def scores(a, b, keep):
        value = dot(a, b, (1, 1))
        if keep is not None:
            value = jnp.where(keep, value, 0.0)
        return value.astype(BF16)

    def total(lefts, rights):
        value = dot(jnp.concatenate(lefts, 1), jnp.concatenate(rights, 0), (1, 0))
        return (value * factor).astype(BF16)

    copies = []

    def store(slot, column, index, tile, value):
        at = pl.ds(tile * TILE, TILE)
        staged[slot, index, at] = value
        copies.append(
            pltpu.make_async_copy(
                staged.at[slot, index, at],
                outputs[index].at[0, at, pl.ds(column * HD, HD)],
                sem.at[slot, index, tile],
            )
        )
        copies[-1].start()

    slot = 0
    for group, (offset, first, heads) in enumerate(groups):
        arrays = refs[group * (parts + 2) :][: parts + 2]
        received, states = arrays[:parts], arrays[parts:]
        for head in range(heads):
            for step, ref in zip(steps_of(parts), received):
                place = source_of(me, step, parts)
                for tensor in range(4):
                    ordered[slot, tensor, place] = ref[4 * head + tensor]
            key_state, query_state = read_states(states, head + offset)
            query_turned = query_state.astype(F32).T.astype(BF16)
            query, keys, values, grads = (
                ordered[slot, tensor].reshape(tiles, TILE, HD) for tensor in range(4)
            )
            for i in range(tiles):
                before, after = range(i + 1), range(i, tiles)
                column = first + head
                store(slot, column, 0, i, total(
                    [scores(grads[i], values[j], low if i == j else None) for j in before] + [grads[i]],
                    [keys[j] for j in before] + [key_state],
                ))
                store(slot, column, 1, i, total(
                    [scores(values[i], grads[j], high if i == j else None) for j in after] + [values[i]],
                    [query[j] for j in after] + [query_turned],
                ))
                store(slot, column, 2, i, total(
                    [scores(keys[i], query[j], high if i == j else None) for j in after] + [keys[i]],
                    [grads[j] for j in after] + [query_state],
                ))
            slot += 1
    for copy in copies:
        copy.wait()
    token[...] = jnp.zeros_like(token)


@jax.named_scope("gradients")
def gradients(groups, held, group, factor):
    parts = len(groups[0][0])
    rows = groups[0][0][0].shape[1]
    length = parts * rows
    heads = sum(item[-1] for item in groups)
    arrays = [value for received, states, *_ in groups for value in (*received, *states)]
    return pl.pallas_call(
        functools.partial(grads_kernel, parts, factor, [item[2:] for item in groups]),
        in_specs=[pl.BlockSpec(memory_space=pltpu.VMEM)] * len(arrays)
        + [pl.BlockSpec(memory_space=pltpu.HBM)] * len(held),
        out_specs=[pl.BlockSpec(memory_space=pltpu.HBM)] * 3 + [pl.BlockSpec(memory_space=pltpu.VMEM)],
        out_shape=[jax.ShapeDtypeStruct((1, length, group), BF16)] * 3
        + [jax.ShapeDtypeStruct((8, HD), F32)],
        scratch_shapes=[
            pltpu.VMEM((heads, 4, parts, rows, HD), BF16),
            pltpu.VMEM((heads, 3, length, HD), BF16),
            pltpu.SemaphoreType.DMA((heads, 3, length // TILE)),
        ],
        input_output_aliases={len(arrays) + index: index for index in range(len(held))},
        compiler_params=PARAMS,
        cost_estimate=cost(1000, 1024),
    )(*arrays, *held)


def shards(query, keys, values, grad_out):
    parts = lax.axis_size("head")
    spans = lax.axis_size("ctx")
    _, rows, full = query.shape
    group = full // parts
    heads = group // HD
    factor = (HD * rows * parts * spans) ** -0.5
    late = max(1, heads // 4)
    middle = (heads - late) // 2
    chunks = [heads - late - middle, middle, late]
    arrays = (query, keys, values, grad_out)
    first = pack_first(arrays, parts, heads, chunks[0], late)
    own, packed = pack_rest(arrays, parts, heads, chunks)

    def exchange(own, values):
        return [own] + [
            send(values[step - 1], "head", lambda index: target_of(index, step, parts))
            for step in steps_of(parts)[1:]
        ]

    received = [exchange(own, first)] + [exchange(values[0], values[1:]) for values in packed]
    early, arrived = exchanged(*own_states(received[0], chunks[0], late, []))
    *held, token = gradients([(received[0], early, 0, 0, chunks[0])], (), group, factor)
    *held, ready = gradients([(received[2], early, chunks[0], heads - late, late)], held, group, factor)
    second, _ = exchanged(*own_states(received[1], middle, 0, [arrived[0]]), [token], [ready])
    *held, _ = gradients([(received[1], second, 0, chunks[0], middle)], held, group, factor)
    return tuple(held)


def solution(mesh):
    spec = P("ctx", "head", None)
    out = P("ctx", None, "head")
    return jax.shard_map(
        shards, mesh=mesh, in_specs=(spec,) * 4, out_specs=(out,) * 3, check_vma=False
    )
```
